256 devices in a mesh: fluid: 8 (over z), inflow: 8 (over y, core), solid: 4 (over x).
Axes of the slice: x: 4, y: 4, z: 8, core: 2. Of those that a mesh axis runs over, the one named last changes fastest.
Arguments:
- state: float32 [4, 4, 32, 128, 1024], P('solid', None, None, 'fluid', 'inflow'), may hold values from -5 to 5
- precursor: bfloat16 [4, 2, 4, 131072], P('solid', None, None, ('fluid', 'inflow')), may hold values from -5 to 5
- inlet_map: int32 [4, 128, 1024], P('solid', 'fluid', 'inflow'), may hold values from 0 to 131071, as said below
- face_cell: int32 [4, 8, 8, 4096], P('solid', 'fluid', 'inflow'), may hold values from 0 to 65535
- face_owner: int32 [4, 8, 8, 4096, 1], P('solid', 'fluid', 'inflow'), may hold values from 0 to 3; in each aligned block of 4096 rows (0 to 4095, 4096 to 8191, ..., all dimensions but the last counted through in order) at most 2048 rows name the same one
- wall_temp: float32 [4, 8, 8, 8, 8192], P('solid', 'fluid', 'inflow'), may hold values from -4 to 4
Outputs:
- new_state: float32 [4, 4, 32, 128, 1024], P('solid', None, None, 'fluid', 'inflow')
- new_wall: float32 [4, 8, 8, 8, 8192], P('solid', 'fluid', 'inflow')
The draws below stay inside these ranges and needn't reach their ends.
Inputs may be any that keep to these rules, and one draw needn't show every extreme that they name: `inlet_map`: for each runner and each block of 16 rows, the block's entries are a permutation of the precursor cells whose row (value // 1024) lies in the same block. `face_cell`: Device-local cell indices; cells may repeat. `face_owner`: in the rows of one device no owner is named by more than 2048 faces; some device names one owner exactly 2048 times.
All inputs are finite; a program needn't handle non-finite values.
Results may differ from the reference program's by a relative error of at most 0.0003.
Values may be sent and summed in bfloat16 or wider, within the bound.
A program may use at most 128 MiB of HBM per device.

```python
import math
import jax
import jax.numpy as jnp
import numpy as np

XL = 32
CY = 16
CZ = 128
NV = 4
STEPS = 2
LAYERS = 8
FACE_DEV = 4096
CAP = 2048
RUNNERS = 4
NY = 128
NZ = 1024
N_FLUID = 8
N_INFLOW = 8
N_SOLID = 4


def draw_inlet_map(key, part):
    block_size = CY * NZ
    key_list = jax.random.split(key, N_SOLID * N_FLUID)
    orders = jax.vmap(lambda one_key: jax.random.permutation(one_key, block_size))(key_list).astype(jnp.int32)
    offsets = jnp.arange(N_SOLID * N_FLUID, dtype=jnp.int32) % N_FLUID * block_size
    return (orders + offsets[:, None]).reshape(N_SOLID, N_FLUID * CY, NZ)


def place_ends(entries, key, least, largest):
    longest = entries.shape.index(max(entries.shape))
    spots = []
    for shift in (0, 1):
        where = [jax.random.randint(jax.random.fold_in(key, axis), (), 0, length) for axis, length in enumerate(entries.shape)]
        where[longest] = (where[longest] + shift) % entries.shape[longest]
        spots.append(tuple(where))
    return entries.at[spots[0]].set(least).at[spots[1]].set(largest)


def block_levels(stream_key, extent, cuts, low, top_value):
    factor_of = 1.0
    for axis_at, blocks in cuts:
        heights = jax.random.uniform(jax.random.fold_in(jax.random.fold_in(stream_key, 6), axis_at), (blocks,), jnp.float32, low / len(cuts), top_value / len(cuts))
        factor_of = factor_of * jnp.repeat(jnp.exp(heights), extent[axis_at] // blocks).reshape((-1,) + (1,) * (len(extent) - 1 - axis_at))
    return factor_of


def routed_block(own_key, own, number, rows, count, top, most, skew):
    order = jax.random.permutation(own_key, count)
    packed, usual = portions_of(count, rows * top, most, skew, True), portions_of(count, rows * top, most, skew, False)
    places = jnp.arange(count)

    def named(tallies, offset_by):
        used = int((tallies > 0).sum())
        fixed = max(1, used // 4)
        passed = fixed + (places - fixed + offset_by * (used - fixed)) % max(1, count - fixed)
        return jnp.zeros((count,), jnp.int32).at[order[jnp.where(places < fixed, places, passed)]].set(jnp.asarray(tallies, jnp.int32))

    tallies = jnp.where(number % 4 == 0, named(packed, number // 4), named(usual, number - number // 4 - 1))
    mixed = jax.random.permutation(jax.random.fold_in(own, 3), count)
    source_of, receiver = mixed[0:count // 2 * 2:2], mixed[1:count // 2 * 2:2]
    room = jnp.minimum(tallies[source_of] - 1, most - tallies[receiver]) // 2
    room = jnp.where((source_of == order[0]) | (receiver == order[0]) | (tallies[receiver] == 0), 0, jnp.maximum(room, 0))
    passed = jax.random.randint(jax.random.fold_in(own, 4), (count // 2,), 0, 1 << 20) % (room + 1)
    tallies = tallies.at[source_of].add(-passed).at[receiver].add(passed)
    labels = jnp.searchsorted(jnp.cumsum(tallies), jnp.arange(rows * top), side="right").astype(jnp.int32)
    table = labels.reshape(top, rows).T
    table = table[jax.random.permutation(jax.random.fold_in(own, 1), rows)]
    offset_by = jax.random.randint(jax.random.fold_in(own, 2), (rows, 1), 0, top)
    return jnp.take_along_axis(table, (jnp.arange(top)[None, :] + offset_by) % top, axis=1)


def portions_of(count, total, bound, lean, full):
    portions = [(1 << 20) // math.isqrt(standing ** lean) + 1 for standing in range(1, count + 1)]
    largest = bound if full else min(bound, max(-(-total // count), total * portions[0] // sum(portions)))
    least = 1 if total - largest >= count - 1 else 0
    holding, rest = [largest] + [least] * (count - 1), total - largest - least * (count - 1)
    while rest > 0:
        movable = [i for i in range(1, count) if holding[i] < largest] or [i for i in range(1, count) if holding[i] < bound]
        whole, remaining = sum([portions[i] for i in movable]), rest
        for i in movable:
            extra = min(bound - holding[i], max(1, remaining * portions[i] // whole), rest)
            holding[i] = holding[i] + extra
            rest = rest - extra
    return np.array(holding)


def centred(rng, dims, scale, limit, pieces=(), kind=jnp.bfloat16):
    factor_of = block_levels(rng, dims, pieces, -0.22, 0.18) if pieces else 1.0
    result = jax.random.normal(rng, dims, jnp.float32) * scale * factor_of
    return jnp.minimum(jnp.maximum(result, -limit), limit).astype(kind)


def setup_inputs(seed: int = 0) -> dict:
    splits = jax.random.split(jax.random.key(seed), 7)
    state = centred(splits[0], (RUNNERS, NV, XL, NY, NZ), 1.0, 5.0, ((0, 4), (3, 8), (4, 8)), jnp.float32)
    precursor = centred(splits[1], (RUNNERS, STEPS, NV, NY * NZ), 1.0, 5.0, ((0, 4), (3, 64)))
    inlet_map = draw_inlet_map(jax.random.fold_in(splits[6], 71), 0)
    face_cell = place_ends(jax.random.randint(splits[3], (RUNNERS, N_FLUID, N_INFLOW, FACE_DEV), 0, XL * CY * CZ), jax.random.fold_in(splits[3], 1), 0, (XL * CY * CZ) - 1).astype(jnp.int32)
    face_owner_keys = jax.random.split(jax.random.fold_in(splits[4], 1), RUNNERS * N_FLUID * N_INFLOW * FACE_DEV // FACE_DEV)
    face_owner_turns = jax.random.permutation(jax.random.fold_in(splits[4], 3), RUNNERS * N_FLUID * N_INFLOW * FACE_DEV // FACE_DEV)
    face_owner = jax.vmap(lambda own, number: routed_block(jax.random.fold_in(splits[4], 2), own, number, FACE_DEV, N_SOLID, 1, CAP, 2))(face_owner_keys, face_owner_turns).reshape((RUNNERS, N_FLUID, N_INFLOW, FACE_DEV, 1))
    wall_temp = centred(splits[5], (RUNNERS, N_FLUID, N_INFLOW, LAYERS, N_SOLID * CAP), 1.0, 4.0, ((0, 4), (1, 8), (2, 8)), jnp.float32)
    return {"state": state, "precursor": precursor, "inlet_map": inlet_map, "face_cell": face_cell, "face_owner": face_owner, "wall_temp": wall_temp}


TIME_STEP = 0.1
VISCOSITY = 0.5
HEAT_TRANSFER = 0.8
CONDUCT_SLOPE = 0.2
SOLID_STEP = 0.15
WALL_WEIGHT = 0.5


def update(flow_field, minus_x, plus_x, minus_y, plus_y, minus_z, plus_z, heat_term):
    laplace = minus_x + plus_x + minus_y + plus_y + minus_z + plus_z - 6.0 * flow_field
    advection = 0.5 * (flow_field[0:1] * (plus_x - minus_x) + flow_field[1:2] * (plus_y - minus_y) + flow_field[2:3] * (plus_z - minus_z))
    updated = flow_field + TIME_STEP * (VISCOSITY * laplace - advection)
    return updated.at[3].add(heat_term)


def conduct(received, valid_in, solid_temps):
    speed_sq = received[..., 0, :] ** 2 + received[..., 1, :] ** 2 + received[..., 2, :] ** 2
    transfer = HEAT_TRANSFER * (1.0 + 0.5 * speed_sq)
    wall_flux = valid_in * transfer * (received[..., 3, :] - solid_temps[..., 0, :])
    conductivity = jnp.exp(CONDUCT_SLOPE * solid_temps)
    interface = 0.5 * (conductivity[..., :-1, :] + conductivity[..., 1:, :]) * (solid_temps[..., 1:, :] - solid_temps[..., :-1, :])
    outermost = conductivity[..., -1:, :] * (0.0 - solid_temps[..., -1:, :])
    from_above = jnp.concatenate([interface, outermost], axis=-2)
    from_below = jnp.concatenate([wall_flux[..., None, :], -interface], axis=-2)
    return wall_flux, solid_temps + SOLID_STEP * (from_above + from_below)


def blocks(flow_field):
    runners, channels = flow_field.shape[0], flow_field.shape[1]
    view = flow_field.reshape(runners, channels, XL, N_FLUID, CY, N_INFLOW, CZ).transpose(0, 3, 5, 1, 2, 4, 6)
    return view.reshape(runners, N_FLUID, N_INFLOW, channels, XL * CY * CZ)


def unblocks(blocked):
    runners, channels = blocked.shape[0], blocked.shape[3]
    view = blocked.reshape(runners, N_FLUID, N_INFLOW, channels, XL, CY, CZ).transpose(0, 3, 4, 1, 5, 2, 6)
    return view.reshape(runners, channels, XL, N_FLUID * CY, N_INFLOW * CZ)


def to_owner(buffer, runners):
    channels = buffer.shape[1]
    view = buffer.reshape(runners, N_FLUID, N_INFLOW, channels, N_SOLID, CAP).transpose(4, 1, 2, 3, 0, 5)
    return view.reshape(runners * N_FLUID * N_INFLOW, channels, N_SOLID * CAP)


def step_runner(flow_field, inlet_plane, heat_term):
    padded = jnp.pad(flow_field, ((0, 0), (0, 0), (1, 1), (1, 1)))
    minus_x = jnp.concatenate([inlet_plane[:, None], flow_field[:, :-1]], axis=1)
    plus_x = jnp.concatenate([flow_field[:, 1:], flow_field[:, -1:]], axis=1)
    return update(flow_field, minus_x, plus_x, padded[:, :, :-2, 1:-1], padded[:, :, 2:, 1:-1], padded[:, :, 1:-1, :-2], padded[:, :, 1:-1, 2:], heat_term)


def reference(state, precursor, inlet_map, face_cell, face_owner, wall_temp):
    runners = state.shape[0]
    device_count = runners * N_FLUID * N_INFLOW
    columns = N_SOLID * CAP
    cell_count = XL * CY * CZ
    maps = inlet_map.reshape(runners, -1)
    planes = jax.vmap(lambda stored, index: stored[:, :, index])(precursor.astype(jnp.float32), maps)
    planes = planes.reshape(runners, STEPS, NV, N_FLUID * CY, N_INFLOW * CZ)
    wall_cells = face_cell.reshape(device_count, FACE_DEV)
    face_owners = face_owner.reshape(device_count, FACE_DEV)
    choose = (face_owners[:, :, None] == jnp.arange(N_SOLID, dtype=jnp.int32)[None, None, :]).astype(jnp.int32)
    face_rank = jnp.sum(choose * (jnp.cumsum(choose, axis=1) - 1), axis=2)
    slot_index = (face_owners * CAP + face_rank).astype(jnp.int32)
    valid_out = jax.vmap(lambda slots: jnp.zeros((columns,), jnp.float32).at[slots].set(1.0))(slot_index)
    valid_in = to_owner(valid_out[:, None, :], runners)[:, 0]
    solid_temps = wall_temp.reshape(device_count, LAYERS, columns)
    flow_field = state
    for step_index in range(STEPS):
        flat_field = blocks(flow_field).reshape(device_count, NV, cell_count)
        values = jax.vmap(lambda block, where: block[:, where])(flat_field, wall_cells)
        send_buffer = jax.vmap(lambda sample, slots: jnp.zeros((NV, columns), jnp.float32).at[:, slots].set(sample))(values, slot_index)
        received = to_owner(send_buffer, runners)
        wall_flux, solid_temps = conduct(received, valid_in, solid_temps)
        returned = to_owner(wall_flux[:, None, :], runners)[:, 0]
        face_flux = jnp.take_along_axis(returned, slot_index, axis=1)
        heat_term = jax.vmap(lambda where, amount: jnp.zeros((cell_count,), jnp.float32).at[where].add(-WALL_WEIGHT * amount))(wall_cells, face_flux)
        heat_field = unblocks(heat_term.reshape(runners, N_FLUID, N_INFLOW, 1, cell_count))[:, 0]
        flow_field = jax.vmap(step_runner)(flow_field, planes[:, step_index], heat_field)
    return flow_field, solid_temps.reshape(wall_temp.shape)
```

```python
import functools

import jax
import jax.numpy as jnp
from jax import lax
from jax.experimental import pallas as pl
from jax.experimental.pallas import tpu as pltpu
from jax.sharding import PartitionSpec as P

F32, BF16, I32 = jnp.float32, jnp.bfloat16, jnp.int32
MESH = pl.DeviceIdType.MESH

XL, CY, CZ, NV = 32, 16, 128, 4
CAP, LAYERS, FACES = 2048, 8, 4096
N_FLUID, N_INFLOW, N_SOLID = 8, 8, 4
COLUMNS = N_SOLID * CAP
ROWS = FACES // 128

TIME_STEP = 0.1
VISCOSITY = 0.5
HEAT_TRANSFER = 0.8
CONDUCT_SLOPE = 0.2
SOLID_STEP = 0.15
WALL_WEIGHT = 0.5


def split(x):
    high = x.astype(BF16)
    return high, (x - high.astype(F32)).astype(BF16)


def transfer_of(u, v, w):
    return HEAT_TRANSFER * (1.0 + 0.5 * (u * u + v * v + w * w))


def iota(shape, dim):
    return lax.broadcasted_iota(I32, shape, dim)


def bits(mask):
    return jnp.where(mask, 1.0, 0.0).astype(BF16)


def dot(a, b):
    return lax.dot_general(a, b, (((1,), (0,)), ((), ())), preferred_element_type=F32)


def dot_t(a, b):
    return lax.dot_general(a, b, (((1,), (1,)), ((), ())), preferred_element_type=F32)


def kernel(
    state,
    prec,
    imap,
    fcell,
    fown,
    wall,
    out_state,
    out_wall,
    q0,
    q1,
    ob,
    wv,
    pv,
    imv,
    fcv,
    fov,
    psend,
    win,
    wsend,
    wrecv,
    hy_send,
    hy_recv,
    hz_send,
    hz_recv,
    fsend,
    frecv,
    oh_cell,
    oh_slot,
    oh_in,
    vm,
    lhs,
    wl,
    kcell,
    rcell,
    kslot,
    rslot,
    kin,
    rin,
    count,
    s_sum,
    i_sum,
    f_sum,
    a_face,
    b_face,
    t_face,
    i_face,
    f_face,
    load_sem,
    p_send_sem,
    p_recv_sem,
    w_send_sem,
    w_recv_sem,
    h_send_sem,
    h_recv_sem,
    f_send_sem,
    f_recv_sem,
    out_sem,
):
    fl, inf, so = lax.axis_index("fluid"), lax.axis_index("inflow"), lax.axis_index("solid")

    loads = [
        pltpu.make_async_copy(prec, pv, load_sem.at[0]),
        pltpu.make_async_copy(wall, wv, load_sem.at[1]),
        pltpu.make_async_copy(state, q0.at[:, pl.ds(1, XL)], load_sem.at[2]),
        pltpu.make_async_copy(fown, fov, load_sem.at[3]),
        pltpu.make_async_copy(fcell, fcv, load_sem.at[4]),
        pltpu.make_async_copy(imap, imv, load_sem.at[5]),
    ]
    for load in loads:
        load.start()

    barrier = pltpu.get_barrier_semaphore()

    def greet(ids):
        pl.semaphore_signal(barrier, inc=1, device_id=ids, device_id_type=MESH)

    for d in range(1, N_INFLOW):
        greet({"inflow": lax.rem(inf + d, N_INFLOW)})
    for d in (1, N_FLUID - 1):
        greet({"fluid": lax.rem(fl + d, N_FLUID)})
    for d in range(1, N_SOLID):
        greet({"solid": lax.rem(so + d, N_SOLID)})

    lane = iota((CY, CZ), 1)
    row = iota((CY, CZ), 0)

    loads[0].wait()
    for s in range(2):
        for k in range(16):
            psend[s, pl.ds(k, 4, stride=16), :] = pv[s, :, k * 128 : (k + 1) * 128].astype(F32)
    for s in range(2):
        win[s, inf] = psend[s].astype(BF16)
    loads[1].wait()
    for t in range(64):
        wsend[pl.ds(t // 16 * 32 + t % 16, 2, stride=16), :] = wv[0:2, t * 128 : (t + 1) * 128]
    loads[2].wait()

    def pack_edges(x, values, packed):
        low, high = packed
        for c in range(NV):
            k = c * XL + x
            low = jnp.where(lane == k, pltpu.roll(values[c], k, 1), low)
            high = jnp.where(lane == k, pltpu.roll(values[c], lax.rem(k + 1, 128), 1), high)
            hy = values[c]
            keep_row(c, x, hy)
        return low, high

    def keep_row(c, x, value):
        k = c * XL + x
        hy_now[0, pl.ds(k, 1), :] = value[0:1]
        hy_now[1, pl.ds(k, 1), :] = value[CY - 1 : CY]

    hy_now = hy_send.at[0]

    def edges_of(x, packed):
        return pack_edges(x, [q0[c, x + 1] for c in range(NV)], packed)

    zero_plane = jnp.zeros((CY, CZ), F32)
    low, high = lax.fori_loop(0, XL, edges_of, (zero_plane, zero_plane))
    hz_send[0, 0] = low
    hz_send[0, 1] = high
    for c in range(NV):
        q0[c, XL + 1] = q0[c, XL]

    pl.semaphore_wait(barrier, (N_INFLOW - 1) + 2 + (N_SOLID - 1))

    wall_copies = []
    for d in range(1, N_SOLID):
        to = lax.rem(so + d, N_SOLID)
        wall_copies.append(
            pltpu.make_async_remote_copy(
                src_ref=wsend.at[pl.ds(pl.multiple_of(to * 32, 32), 32)],
                dst_ref=wrecv.at[pl.ds(pl.multiple_of(so * 32, 32), 32)],
                send_sem=w_send_sem.at[d - 1],
                recv_sem=w_recv_sem.at[d - 1],
                device_id={"solid": to},
                device_id_type=MESH,
            )
        )

    def halo_copies(step):
        copies = []
        for side in range(2):
            far = N_FLUID - 1 if side == 0 else 1
            copies.append(
                pltpu.make_async_remote_copy(
                    src_ref=hy_send.at[step, side],
                    dst_ref=hy_recv.at[step, 1 - side],
                    send_sem=h_send_sem.at[step, 0, side],
                    recv_sem=h_recv_sem.at[step, 0, side],
                    device_id={"fluid": lax.rem(fl + far, N_FLUID)},
                    device_id_type=MESH,
                )
            )
        for side in range(2):
            far = N_INFLOW - 1 if side == 0 else 1
            copies.append(
                pltpu.make_async_remote_copy(
                    src_ref=hz_send.at[step, side],
                    dst_ref=hz_recv.at[step, 1 - side],
                    send_sem=h_send_sem.at[step, 1, side],
                    recv_sem=h_recv_sem.at[step, 1, side],
                    device_id={"inflow": lax.rem(inf + far, N_INFLOW)},
                    device_id_type=MESH,
                )
            )
        return copies

    def precursor_copies(step):
        return [
            pltpu.make_async_remote_copy(
                src_ref=win.at[step, inf],
                dst_ref=win.at[step, inf],
                send_sem=p_send_sem.at[step, d - 1],
                recv_sem=p_recv_sem.at[step, d - 1],
                device_id={"inflow": lax.rem(inf + d, N_INFLOW)},
                device_id_type=MESH,
            )
            for d in range(1, N_INFLOW)
        ]

    def precursor_arrivals(step):
        for d in range(1, N_INFLOW):
            came = lax.rem(inf + N_INFLOW - d, N_INFLOW)
            pltpu.make_async_remote_copy(
                src_ref=win.at[step, came],
                dst_ref=win.at[step, came],
                send_sem=p_send_sem.at[step, d - 1],
                recv_sem=p_recv_sem.at[step, d - 1],
                device_id={"inflow": came},
                device_id_type=MESH,
            ).wait_recv()

    def wall_arrivals():
        for d in range(1, N_SOLID):
            came = lax.rem(so + N_SOLID - d, N_SOLID)
            pltpu.make_async_remote_copy(
                src_ref=wsend.at[pl.ds(pl.multiple_of(came * 32, 32), 32)],
                dst_ref=wrecv.at[pl.ds(pl.multiple_of(came * 32, 32), 32)],
                send_sem=w_send_sem.at[d - 1],
                recv_sem=w_recv_sem.at[d - 1],
                device_id={"solid": came},
                device_id_type=MESH,
            ).wait_recv()

    def flux_copies(step):
        copies = []
        for d in range(1, N_SOLID):
            to = lax.rem(so + d, N_SOLID)
            copies.append(
                pltpu.make_async_remote_copy(
                    src_ref=fsend.at[step, pl.ds(pl.multiple_of(to * 16, 16), 16)],
                    dst_ref=frecv.at[step, pl.ds(pl.multiple_of(so * 16, 16), 16)],
                    send_sem=f_send_sem.at[step, d - 1],
                    recv_sem=f_recv_sem.at[step, d - 1],
                    device_id={"solid": to},
                    device_id_type=MESH,
                )
            )
        return copies

    def flux_arrivals(step):
        for d in range(1, N_SOLID):
            came = lax.rem(so + N_SOLID - d, N_SOLID)
            pltpu.make_async_remote_copy(
                src_ref=fsend.at[step, pl.ds(pl.multiple_of(came * 16, 16), 16)],
                dst_ref=frecv.at[step, pl.ds(pl.multiple_of(came * 16, 16), 16)],
                send_sem=f_send_sem.at[step, d - 1],
                recv_sem=f_recv_sem.at[step, d - 1],
                device_id={"solid": came},
                device_id_type=MESH,
            ).wait_recv()

    sent = wall_copies + halo_copies(0) + precursor_copies(0) + precursor_copies(1)
    halos_0 = sent[N_SOLID - 1 : N_SOLID + 3]
    for copy in sent:
        copy.start()

    for load in loads[3:]:
        load.wait()
    cell = fcv[...]
    kcell[...] = lax.shift_right_logical(cell, 14) * 128 + (cell & 127)
    rcell[...] = lax.shift_right_logical(cell, 7) & 127
    owner = fov[...]
    marks = jnp.concatenate([jnp.where(owner == o, 1.0, 0.0) for o in range(N_SOLID)], axis=0)
    upper = jnp.where(iota((128, 128), 0) < iota((128, 128), 1), 1.0, 0.0)
    earlier = dot(
        marks.astype(BF16), jnp.concatenate([upper, jnp.ones((128, 128), F32)], axis=1).astype(BF16)
    )
    r_out, r_in = iota((128, 128), 0), iota((128, 128), 1)
    same = lax.shift_right_logical(r_out, 5) == lax.shift_right_logical(r_in, 5)
    below = bits(jnp.logical_and(same, r_in < r_out))
    ranks = (earlier[:, :128] + dot(below, earlier[:, 128:].astype(BF16))) * marks
    rank = ranks[0:32] + ranks[32:64] + ranks[64:96] + ranks[96:128]
    slot = owner * CAP + rank.astype(I32)
    hi = lax.shift_right_logical(slot, 7)
    kslot[...] = lax.shift_right_logical(hi, 5) * 128 + (slot & 127)
    rslot[...] = hi & 31
    relative = imv[...] - fl * (N_INFLOW * CAP)
    hi = lax.shift_right_logical(relative, 7)
    kin[...] = lax.shift_right_logical(hi, 6) * 128 + (relative & 127)
    rin[...] = hi & 63

    for j in range(ROWS):
        oh_cell[:, j * 128 : (j + 1) * 128] = bits(iota((512, 128), 0) == kcell[j : j + 1, :])
    for j in range(ROWS):
        oh_slot[:, j * 128 : (j + 1) * 128] = bits(iota((256, 128), 0) == kslot[j : j + 1, :])
    for j in range(CY):
        oh_in[:, j * 128 : (j + 1) * 128] = bits(iota((256, 128), 0) == kin[j : j + 1, :])

    def scatter_cells(fields):
        for j in range(ROWS):
            mask = iota((128, 128), 0) == rcell[j : j + 1, :]
            for i, field in enumerate(fields):
                vm[i * 128 : (i + 1) * 128, j * 128 : (j + 1) * 128] = jnp.where(
                    mask, field[j : j + 1, :], 0.0
                ).astype(BF16)
        return dot_t(vm[0 : len(fields) * 128, :], oh_cell[...])

    def halves(x):
        high, low = split(x)
        return high.astype(F32), low.astype(F32)

    count[...] = scatter_cells([jnp.ones((ROWS, 128), F32)])

    def store_sample_plane(quarter, xr, u, v, w, temp):
        at = pl.multiple_of(xr * CY, CY)
        parts = split(transfer_of(u, v, w)) + split(temp)
        for i, part in enumerate(parts):
            lhs[pl.ds(i * 128 + at, CY), quarter * 128 : (quarter + 1) * 128] = part

    def sample_faces():
        def chunk(n, _):
            cols = oh_cell[:, pl.ds(pl.multiple_of(n * 512, 512), 512)]
            found = dot(lhs[...], cols)
            for j in range(4):
                at = n * 4 + j
                mask = iota((128, 128), 0) == rcell[pl.ds(at, 1), :]
                part = found[:, j * 128 : (j + 1) * 128]
                for ref, base in ((a_face, 0), (b_face, 256)):
                    both = part[base : base + 128] + part[base + 128 : base + 256]
                    ref[pl.ds(at, 1), :] = jnp.sum(jnp.where(mask, both, 0.0), axis=0, keepdims=True)
            return 0

        lax.fori_loop(0, FACES // 512, chunk, 0)

    for quarter in range(4):

        def plane(xr, _):
            x = quarter * 8 + xr
            store_sample_plane(quarter, xr, *[q0[c, x + 1] for c in range(NV)])
            return 0

        lax.fori_loop(0, 8, plane, 0)
    sample_faces()

    own = pl.multiple_of(so * 32, 32)
    wrecv[pl.ds(own, 32)] = wsend[pl.ds(own, 32)]
    wall_arrivals()
    for o in range(N_SOLID):
        for layer in range(2):
            for i, part in enumerate(split(wrecv[o * 32 + layer * 16 : o * 32 + layer * 16 + 16, :])):
                at = (layer * 2 + i) * 32 + (o & 1) * 16
                wl[at : at + 16, (o >> 1) * 128 : (o >> 1) * 128 + 128] = part

    def wall_chunk(n, _):
        cols = oh_slot[:, pl.ds(pl.multiple_of(n * 512, 512), 512)]
        found = dot(wl[...], cols)
        for j in range(4):
            at = n * 4 + j
            mask = iota((32, 128), 0) == rslot[pl.ds(at, 1), :]
            part = found[:, j * 128 : (j + 1) * 128]
            for ref, base in ((t_face, 0), (i_face, 64)):
                both = part[base : base + 32] + part[base + 32 : base + 64]
                ref[pl.ds(at, 1), :] = jnp.sum(jnp.where(mask, both, 0.0), axis=0, keepdims=True)
        return 0

    lax.fori_loop(0, FACES // 512, wall_chunk, 0)
    t0 = t_face[...]
    t1 = i_face[...]
    i_face[...] = (
        0.5 * (jnp.exp(CONDUCT_SLOPE * t0) + jnp.exp(CONDUCT_SLOPE * t1)) * (t1 - t0)
    )

    sums = scatter_cells(halves(t_face[...]))
    s_sum[...] = sums[0:128] + sums[128:256]

    def inlet(step, dst):
        for g in range(CY // 4):
            window = jnp.concatenate(
                [win[step, 0:4].reshape(256, 128), win[step, 4:8].reshape(256, 128)], axis=1
            )
            found = dot(window, oh_in[:, g * 512 : (g + 1) * 512])
            for j in range(4):
                y = g * 4 + j
                index = rin[y : y + 1, :]
                part = found[:, j * 128 : (j + 1) * 128]
                for c in range(NV):
                    total = None
                    for src in range(4):
                        mask = iota((16, 128), 0) + src * 16 == index
                        term = jnp.where(mask, part[src * 64 + c * 16 : src * 64 + c * 16 + 16], 0.0)
                        total = term if total is None else total + term
                    dst[c, 0, y : y + 1, :] = jnp.sum(total, axis=0, keepdims=True)

    precursor_arrivals(0)
    inlet(0, q0)

    def neighbours(src, hy, zlow, zhigh, x, c, q):
        k = c * XL + x
        y_low = jnp.where(fl > 0, hy[0, pl.ds(k, 1), :], 0.0)
        y_high = jnp.where(fl < N_FLUID - 1, hy[1, pl.ds(k, 1), :], 0.0)
        minus_y = jnp.where(row == 0, y_low, pltpu.roll(q, 1, 0))
        plus_y = jnp.where(row == CY - 1, y_high, pltpu.roll(q, CY - 1, 0))
        minus_z = jnp.where(
            lane == 0, pltpu.roll(zlow, lax.rem(128 - k, 128), 1), pltpu.roll(q, 1, 1)
        )
        plus_z = jnp.where(lane == CZ - 1, pltpu.roll(zhigh, 127 - k, 1), pltpu.roll(q, CZ - 1, 1))
        return src[c, x], src[c, x + 2], minus_y, plus_y, minus_z, plus_z

    def advanced(src, hy, zlow, zhigh, x):
        centre = [src[c, x + 1] for c in range(NV)]
        u, v, w, _ = centre
        fresh = []
        for c in range(NV):
            q = centre[c]
            xm, xp, ym, yp, zm, zp = neighbours(src, hy, zlow, zhigh, x, c, q)
            laplace = xm + xp + ym + yp + zm + zp - 6.0 * q
            advection = 0.5 * (u * (xp - xm) + v * (yp - ym) + w * (zp - zm))
            fresh.append(q + TIME_STEP * (VISCOSITY * laplace - advection))
        return centre, fresh

    for copy in halos_0:
        copy.wait_recv()
    zlow_0 = jnp.where(inf > 0, hz_recv[0, 0], 0.0)
    zhigh_0 = jnp.where(inf < N_INFLOW - 1, hz_recv[0, 1], 0.0)
    hy_now = hy_send.at[1]
    packed = (zero_plane, zero_plane)
    for quarter in range(4):

        def first(xr, packed):
            x = quarter * 8 + xr
            at = pl.multiple_of(xr * CY, CY)
            cols = slice(quarter * 128, (quarter + 1) * 128)
            centre, fresh = advanced(q0, hy_recv.at[0], zlow_0, zhigh_0, x)
            u, v, w, temp = centre
            total = transfer_of(u, v, w) * (
                count[pl.ds(at, CY), cols] * temp - s_sum[pl.ds(at, CY), cols]
            )
            f_sum[pl.ds(at, CY), cols] = total
            fresh[3] = fresh[3] - WALL_WEIGHT * total
            for c in range(NV):
                q1[c, x + 1] = fresh[c]
            store_sample_plane(quarter, xr, *fresh)
            return pack_edges(x, fresh, packed)

        packed = lax.fori_loop(0, 8, first, packed)
    hz_send[1, 0] = packed[0]
    hz_send[1, 1] = packed[1]
    halos_1 = halo_copies(1)
    for copy in halos_1:
        copy.start()
    for c in range(NV):
        q1[c, XL + 1] = q1[c, XL]

    def send_flux(step, flux):
        parts = halves(flux)
        for j in range(ROWS):
            mask = iota((32, 128), 0) == rslot[j : j + 1, :]
            for i, part in enumerate(parts):
                vm[i * 32 : (i + 1) * 32, j * 128 : (j + 1) * 128] = jnp.where(
                    mask, part[j : j + 1, :], 0.0
                ).astype(BF16)
        found = dot_t(vm[0:64, :], oh_slot[...])
        both = found[0:32] + found[32:64]
        for o in range(N_SOLID):
            fsend[step, o * 16 : (o + 1) * 16] = both[
                (o & 1) * 16 : (o & 1) * 16 + 16, (o >> 1) * 128 : (o >> 1) * 128 + 128
            ]
        copies = flux_copies(step)
        for copy in copies:
            copy.start()
        own = pl.multiple_of(so * 16, 16)
        frecv[step, pl.ds(own, 16)] = fsend[step, pl.ds(own, 16)]
        return copies

    flux = a_face[...] * (b_face[...] - t_face[...])
    f_face[...] = flux
    flux_0 = send_flux(0, flux)

    sample_faces()
    t_later = t_face[...] + SOLID_STEP * (i_face[...] + f_face[...])
    flux_1 = send_flux(1, a_face[...] * (b_face[...] - t_later))

    sums = scatter_cells(halves(i_face[...]))
    i_sum[...] = s_sum[...] + SOLID_STEP * (sums[0:128] + sums[128:256] + f_sum[...])

    precursor_arrivals(1)
    inlet(1, q1)
    for copy in halos_1:
        copy.wait_recv()
    zlow_1 = jnp.where(inf > 0, hz_recv[1, 0], 0.0)
    zhigh_1 = jnp.where(inf < N_INFLOW - 1, hz_recv[1, 1], 0.0)
    outs = []
    for quarter in range(4):

        def second(xr, _):
            x = quarter * 8 + xr
            at = pl.multiple_of(xr * CY, CY)
            cols = slice(quarter * 128, (quarter + 1) * 128)
            centre, fresh = advanced(q1, hy_recv.at[1], zlow_1, zhigh_1, x)
            u, v, w, temp = centre
            total = transfer_of(u, v, w) * (
                count[pl.ds(at, CY), cols] * temp - i_sum[pl.ds(at, CY), cols]
            )
            fresh[3] = fresh[3] - WALL_WEIGHT * total
            for c in range(NV):
                ob[c, x] = fresh[c]
            return 0

        lax.fori_loop(0, 8, second, 0)
        out = pltpu.make_async_copy(
            ob.at[:, pl.ds(quarter * 8, 8)],
            out_state.at[:, pl.ds(quarter * 8, 8)],
            out_sem.at[quarter],
        )
        out.start()
        outs.append(out)

    layer = iota((LAYERS, 128), 0)

    def conduct(temps, flux_row):
        conductivity = jnp.exp(CONDUCT_SLOPE * temps)
        above = pltpu.roll(temps, LAYERS - 1, 0)
        c_above = pltpu.roll(conductivity, LAYERS - 1, 0)
        flow = jnp.where(
            layer == LAYERS - 1,
            conductivity * (0.0 - temps),
            0.5 * (conductivity + c_above) * (above - temps),
        )
        from_below = jnp.where(layer == 0, flux_row, -pltpu.roll(flow, 1, 0))
        return temps + SOLID_STEP * (flow + from_below)

    flux_arrivals(0)
    flux_arrivals(1)

    def wall_tile(t, _):
        cols = pl.ds(pl.multiple_of(t * 128, 128), 128)
        temps = conduct(wv[:, cols], frecv[0, pl.ds(t, 1), :])
        wv[:, cols] = conduct(temps, frecv[1, pl.ds(t, 1), :])
        return 0

    lax.fori_loop(0, COLUMNS // 128, wall_tile, 0, unroll=4)
    out = pltpu.make_async_copy(wv, out_wall, out_sem.at[4])
    out.start()
    outs.append(out)
    for copy in sent + halos_1 + flux_0 + flux_1:
        copy.wait_send()
    for out in outs:
        out.wait()


def local(state, precursor, inlet_map, face_cell, face_owner, wall_temp):
    any_space = pl.BlockSpec(memory_space=pl.ANY)
    vmem = pltpu.VMEM
    dma = pltpu.SemaphoreType.DMA
    new_state, new_wall = pl.pallas_call(
        kernel,
        out_shape=(
            jax.ShapeDtypeStruct((NV, XL, CY, CZ), F32),
            jax.ShapeDtypeStruct((LAYERS, COLUMNS), F32),
        ),
        in_specs=[any_space] * 6,
        out_specs=(any_space, any_space),
        scratch_shapes=[
            vmem((NV, XL + 2, CY, CZ), F32),
            vmem((NV, XL + 2, CY, CZ), F32),
            vmem((NV, XL, CY, CZ), F32),
            vmem((LAYERS, COLUMNS), F32),
            vmem((2, NV, CAP), BF16),
            vmem((CY, CZ), I32),
            vmem((ROWS, 128), I32),
            vmem((ROWS, 128), I32),
            vmem((2, 64, 128), F32),
            vmem((2, N_INFLOW, 64, 128), BF16),
            vmem((128, 128), F32),
            vmem((128, 128), F32),
            vmem((2, 2, 128, 128), F32),
            vmem((2, 2, 128, 128), F32),
            vmem((2, 2, CY, 128), F32),
            vmem((2, 2, CY, 128), F32),
            vmem((2, 64, 128), F32),
            vmem((2, 64, 128), F32),
            vmem((512, FACES), BF16),
            vmem((256, FACES), BF16),
            vmem((256, CY * CZ), BF16),
            vmem((256, FACES), BF16),
            vmem((512, 512), BF16),
            vmem((128, 256), BF16),
            vmem((ROWS, 128), I32),
            vmem((ROWS, 128), I32),
            vmem((ROWS, 128), I32),
            vmem((ROWS, 128), I32),
            vmem((CY, 128), I32),
            vmem((CY, 128), I32),
            vmem((128, 512), F32),
            vmem((128, 512), F32),
            vmem((128, 512), F32),
            vmem((128, 512), F32),
            vmem((ROWS, 128), F32),
            vmem((ROWS, 128), F32),
            vmem((ROWS, 128), F32),
            vmem((ROWS, 128), F32),
            vmem((ROWS, 128), F32),
            dma((6,)),
            dma((2, N_INFLOW - 1)),
            dma((2, N_INFLOW - 1)),
            dma((N_SOLID - 1,)),
            dma((N_SOLID - 1,)),
            dma((2, 2, 2)),
            dma((2, 2, 2)),
            dma((2, N_SOLID - 1)),
            dma((2, N_SOLID - 1)),
            dma((5,)),
        ],
        compiler_params=pltpu.CompilerParams(
            collective_id=0, has_side_effects=True, vmem_limit_bytes=48 * 1024 * 1024
        ),
        name="manifold_step",
    )(
        state[0],
        precursor[0],
        inlet_map[0],
        face_cell.reshape(ROWS, 128),
        face_owner.reshape(ROWS, 128),
        wall_temp[0, 0, 0],
    )
    return new_state[None], new_wall[None, None, None]


def solution(mesh):
    return jax.shard_map(
        local,
        mesh=mesh,
        in_specs=(
            P("solid", None, None, "fluid", "inflow"),
            P("solid", None, None, ("fluid", "inflow")),
            P("solid", "fluid", "inflow"),
            P("solid", "fluid", "inflow", None),
            P("solid", "fluid", "inflow", None, None),
            P("solid", "fluid", "inflow", None, None),
        ),
        out_specs=(
            P("solid", None, None, "fluid", "inflow"),
            P("solid", "fluid", "inflow", None, None),
        ),
        check_vma=False,
    )
```

```python
import functools

import jax
import jax.numpy as jnp
from jax import lax
from jax.experimental import pallas as pl
from jax.experimental.pallas import tpu as pltpu
from jax.sharding import PartitionSpec as P

F32, BF16, I32 = jnp.float32, jnp.bfloat16, jnp.int32
MESH = pl.DeviceIdType.MESH

XL, CY, CZ, NV = 32, 16, 128, 4
CAP, LAYERS, FACES = 2048, 8, 4096
N_FLUID, N_INFLOW, N_SOLID = 8, 8, 4
COLUMNS = N_SOLID * CAP
ROWS = FACES // 128
TOP, PITCH = 8, 32

TIME_STEP = 0.1
VISCOSITY = 0.5
HEAT_TRANSFER = 0.8
CONDUCT_SLOPE = 0.2
SOLID_STEP = 0.15
WALL_WEIGHT = 0.5


def split(x):
    high = x.astype(BF16)
    return high, (x - high.astype(F32)).astype(BF16)


def transfer_of(u, v, w):
    return HEAT_TRANSFER * (1.0 + 0.5 * (u * u + v * v + w * w))


def iota(shape, dim):
    return lax.broadcasted_iota(I32, shape, dim)


def bits(mask):
    return jnp.where(mask, 1.0, 0.0).astype(BF16)


def dot(a, b):
    return lax.dot_general(a, b, (((1,), (0,)), ((), ())), preferred_element_type=F32)


def dot_t(a, b):
    return lax.dot_general(a, b, (((1,), (1,)), ((), ())), preferred_element_type=F32)


def kernel(
    state,
    prec,
    imap,
    fcell,
    fown,
    wall,
    out_state,
    out_wall,
    q0,
    q1,
    ob,
    wv,
    pv,
    imv,
    fcv,
    fov,
    psend,
    win,
    wsend,
    wrecv,
    hy_send,
    hy_recv,
    hz_send,
    hz_recv,
    fsend,
    frecv,
    oh_cell,
    oh_slot,
    oh_in,
    oh_srow,
    vm,
    lhs,
    wl,
    zf,
    qf,
    rf,
    lf,
    hf,
    sf,
    zi,
    hi_in,
    ri,
    rcell,
    rslot,
    count,
    s_sum,
    i_sum,
    a_face,
    b_face,
    t_face,
    i_face,
    load_sem,
    p_send_sem,
    p_recv_sem,
    w_send_sem,
    w_recv_sem,
    h_send_sem,
    h_recv_sem,
    f_send_sem,
    f_recv_sem,
    out_sem,
):
    fl, inf, so = lax.axis_index("fluid"), lax.axis_index("inflow"), lax.axis_index("solid")

    loads = [
        pltpu.make_async_copy(prec, pv, load_sem.at[0]),
        pltpu.make_async_copy(wall, wv, load_sem.at[1]),
        pltpu.make_async_copy(state, q0.at[:, pl.ds(1, XL), pl.ds(TOP, CY)], load_sem.at[2]),
        pltpu.make_async_copy(fown, fov, load_sem.at[3]),
        pltpu.make_async_copy(fcell, fcv, load_sem.at[4]),
        pltpu.make_async_copy(imap, imv, load_sem.at[5]),
    ]
    for load in loads:
        load.start()

    barrier = pltpu.get_barrier_semaphore()

    def greet(ids):
        pl.semaphore_signal(barrier, inc=1, device_id=ids, device_id_type=MESH)

    for d in range(1, N_INFLOW):
        greet({"inflow": lax.rem(inf + d, N_INFLOW)})
    for d in (1, N_FLUID - 1):
        greet({"fluid": lax.rem(fl + d, N_FLUID)})
    for d in range(1, N_SOLID):
        greet({"solid": lax.rem(so + d, N_SOLID)})

    lane = iota((CY, CZ), 1)

    loads[0].wait()
    for s in range(2):
        for k in range(16):
            psend[s, pl.ds(k, 4, stride=16), :] = pv[s, :, k * 128 : (k + 1) * 128].astype(F32)
    for s in range(2):
        win[s, inf] = psend[s].astype(BF16)
    loads[1].wait()
    for t in range(64):
        wsend[pl.ds(t // 16 * 32 + t % 16, 2, stride=16), :] = wv[0:2, t * 128 : (t + 1) * 128]

    wall_copies = []
    for d in range(1, N_SOLID):
        to = lax.rem(so + d, N_SOLID)
        wall_copies.append(
            pltpu.make_async_remote_copy(
                src_ref=wsend.at[pl.ds(pl.multiple_of(to * 32, 32), 32)],
                dst_ref=wrecv.at[pl.ds(pl.multiple_of(so * 32, 32), 32)],
                send_sem=w_send_sem.at[d - 1],
                recv_sem=w_recv_sem.at[d - 1],
                device_id={"solid": to},
                device_id_type=MESH,
            )
        )

    def halo_copies(step):
        copies = []
        for side in range(2):
            far = N_FLUID - 1 if side == 0 else 1
            copies.append(
                pltpu.make_async_remote_copy(
                    src_ref=hy_send.at[step, side],
                    dst_ref=hy_recv.at[step, 1 - side],
                    send_sem=h_send_sem.at[step, 0, side],
                    recv_sem=h_recv_sem.at[step, 0, side],
                    device_id={"fluid": lax.rem(fl + far, N_FLUID)},
                    device_id_type=MESH,
                )
            )
        for side in range(2):
            far = N_INFLOW - 1 if side == 0 else 1
            copies.append(
                pltpu.make_async_remote_copy(
                    src_ref=hz_send.at[step],
                    dst_ref=hz_recv.at[step, 1 - side],
                    send_sem=h_send_sem.at[step, 1, side],
                    recv_sem=h_recv_sem.at[step, 1, side],
                    device_id={"inflow": lax.rem(inf + far, N_INFLOW)},
                    device_id_type=MESH,
                )
            )
        return copies

    precursor_copies = [
        pltpu.make_async_remote_copy(
            src_ref=win.at[:, inf],
            dst_ref=win.at[:, inf],
            send_sem=p_send_sem.at[d - 1],
            recv_sem=p_recv_sem.at[d - 1],
            device_id={"inflow": lax.rem(inf + d, N_INFLOW)},
            device_id_type=MESH,
        )
        for d in range(1, N_INFLOW)
    ]

    def precursor_arrivals():
        for d in range(1, N_INFLOW):
            came = lax.rem(inf + N_INFLOW - d, N_INFLOW)
            pltpu.make_async_remote_copy(
                src_ref=win.at[:, came],
                dst_ref=win.at[:, came],
                send_sem=p_send_sem.at[d - 1],
                recv_sem=p_recv_sem.at[d - 1],
                device_id={"inflow": came},
                device_id_type=MESH,
            ).wait_recv()

    def wall_arrivals():
        for d in range(1, N_SOLID):
            came = lax.rem(so + N_SOLID - d, N_SOLID)
            pltpu.make_async_remote_copy(
                src_ref=wsend.at[pl.ds(pl.multiple_of(came * 32, 32), 32)],
                dst_ref=wrecv.at[pl.ds(pl.multiple_of(came * 32, 32), 32)],
                send_sem=w_send_sem.at[d - 1],
                recv_sem=w_recv_sem.at[d - 1],
                device_id={"solid": came},
                device_id_type=MESH,
            ).wait_recv()

    flux_copies = []
    for d in range(1, N_SOLID):
        to = lax.rem(so + d, N_SOLID)
        flux_copies.append(
            pltpu.make_async_remote_copy(
                src_ref=fsend.at[:, pl.ds(pl.multiple_of(to * 16, 16), 16)],
                dst_ref=frecv.at[:, pl.ds(pl.multiple_of(so * 16, 16), 16)],
                send_sem=f_send_sem.at[d - 1],
                recv_sem=f_recv_sem.at[d - 1],
                device_id={"solid": to},
                device_id_type=MESH,
            )
        )

    def flux_arrivals():
        for d in range(1, N_SOLID):
            came = lax.rem(so + N_SOLID - d, N_SOLID)
            pltpu.make_async_remote_copy(
                src_ref=fsend.at[:, pl.ds(pl.multiple_of(came * 16, 16), 16)],
                dst_ref=frecv.at[:, pl.ds(pl.multiple_of(came * 16, 16), 16)],
                send_sem=f_send_sem.at[d - 1],
                recv_sem=f_recv_sem.at[d - 1],
                device_id={"solid": came},
                device_id_type=MESH,
            ).wait_recv()

    pl.semaphore_wait(barrier, (N_INFLOW - 1) + 2 + (N_SOLID - 1))
    for copy in wall_copies + precursor_copies:
        copy.start()

    def pair_of(c, x):
        return (c % 2) * XL + x

    def keep_edges(step, x, values, packed):
        packed = list(packed)
        for c in range(NV):
            k = c * XL + x
            hy_send[step, 0, pl.ds(k, 1), :] = values[c][0:1]
            hy_send[step, 1, pl.ds(k, 1), :] = values[c][CY - 1 : CY]
            j = pair_of(c, x)
            moved = pltpu.roll(values[c], 2 * j + 1, 1)
            packed[c // 2] = jnp.where(lax.shift_right_logical(lane, 1) == j, moved, packed[c // 2])
        return tuple(packed)

    zero_plane = jnp.zeros((CY, CZ), F32)
    loads[2].wait()

    def edges_of(x, packed):
        values = [q0[c, x + 1, TOP : TOP + CY, :] for c in range(NV)]
        keep_sample_plane(x, *values)
        return keep_edges(0, x, values, packed)

    def keep_sample_plane(x, u, v, w, temp):
        parts = split(transfer_of(u, v, w)) + split(temp)
        quarter = lax.shift_right_logical(x, 3)
        at = pl.multiple_of((x & 7) * CY, CY)
        for i, part in enumerate(parts):
            lhs[quarter, pl.ds(i * 128 + at, CY), :] = part

    packed = lax.fori_loop(0, XL, edges_of, (zero_plane, zero_plane), unroll=4)
    hz_send[0, 0] = packed[0]
    hz_send[0, 1] = packed[1]
    halos_0 = halo_copies(0)
    for copy in halos_0:
        copy.start()
    for c in range(NV):
        q0[c, XL + 1, TOP : TOP + CY, :] = q0[c, XL, TOP : TOP + CY, :]

    for load in loads[3:]:
        load.wait()
    cell = fcv[...]
    qf[...] = lax.shift_right_logical(cell, 14).astype(F32)
    zf[...] = (cell & 127).astype(F32)
    r = lax.shift_right_logical(cell, 7) & 127
    rcell[...] = r
    rf[...] = r.astype(F32)
    owner = fov[...]
    marks = jnp.concatenate([jnp.where(owner == o, 1.0, 0.0) for o in range(N_SOLID)], axis=0)
    upper = jnp.where(iota((128, 128), 0) < iota((128, 128), 1), 1.0, 0.0)
    earlier = dot(
        marks.astype(BF16), jnp.concatenate([upper, jnp.ones((128, 128), F32)], axis=1).astype(BF16)
    )
    r_out, r_in = iota((128, 128), 0), iota((128, 128), 1)
    same = lax.shift_right_logical(r_out, 5) == lax.shift_right_logical(r_in, 5)
    below = bits(jnp.logical_and(same, r_in < r_out))
    ranks = (earlier[:, :128] + dot(below, earlier[:, 128:].astype(BF16))) * marks
    rank = ranks[0:32] + ranks[32:64] + ranks[64:96] + ranks[96:128]
    slot = owner * CAP + rank.astype(I32)
    hi = lax.shift_right_logical(slot, 7)
    hf[...] = lax.shift_right_logical(hi, 5).astype(F32)
    lf[...] = (slot & 127).astype(F32)
    rslot[...] = hi & 31
    sf[...] = (hi & 31).astype(F32)
    relative = imv[...] - fl * (N_INFLOW * CAP)
    hi = lax.shift_right_logical(relative, 7)
    zi[...] = (relative & 127).astype(F32)
    hi_in[...] = lax.shift_right_logical(hi, 6).astype(F32)
    ri[...] = hi & 63

    steps_128 = iota((128, 128), 0).astype(F32).astype(BF16)
    one, zero = jnp.ones((), BF16), jnp.zeros((), BF16)

    def wide(row_values, blocks):
        tile = jnp.broadcast_to(row_values, (16, 128)).astype(BF16)
        return jnp.concatenate([tile] * blocks, axis=0) if blocks > 1 else tile

    def hot(row_values, blocks):
        return jnp.where(steps_128[: blocks * 16] == wide(row_values, blocks), one, zero)

    def marked(row_values, value, blocks):
        return wide(jnp.where(row_values == value, 1.0, 0.0), blocks)

    for j in range(ROWS):
        cols = slice(j * 128, (j + 1) * 128)
        base = hot(zf[j : j + 1, :], 8)
        for part in range(4):
            oh_cell[part * 128 : (part + 1) * 128, cols] = base * marked(
                qf[j : j + 1, :], float(part), 8
            )
        vm[0:128, cols] = hot(rf[j : j + 1, :], 8)
    for j in range(ROWS):
        cols = slice(j * 128, (j + 1) * 128)
        base = hot(lf[j : j + 1, :], 8)
        for part in range(2):
            oh_slot[part * 128 : (part + 1) * 128, cols] = base * marked(
                hf[j : j + 1, :], float(part), 8
            )
        oh_srow[:, cols] = hot(sf[j : j + 1, :], 2)
    for j in range(CY):
        cols = slice(j * 128, (j + 1) * 128)
        base = hot(zi[j : j + 1, :], 8)
        for part in range(2):
            oh_in[part * 128 : (part + 1) * 128, cols] = base * marked(
                hi_in[j : j + 1, :], float(part), 8
            )

    def sample_faces():
        fields = jnp.concatenate([lhs[i] for i in range(4)], axis=1)

        def chunk(n, _):
            cols = oh_cell[:, pl.ds(pl.multiple_of(n * 512, 512), 512)]
            found = dot(fields, cols)
            for j in range(4):
                at = n * 4 + j
                mask = iota((128, 128), 0) == rcell[pl.ds(at, 1), :]
                part = found[:, j * 128 : (j + 1) * 128]
                for ref, base in ((a_face, 0), (b_face, 256)):
                    both = part[base : base + 128] + part[base + 128 : base + 256]
                    ref[pl.ds(at, 1), :] = jnp.sum(jnp.where(mask, both, 0.0), axis=0, keepdims=True)
            return 0

        lax.fori_loop(0, FACES // 512, chunk, 0, unroll=2)

    sample_faces()

    own = pl.multiple_of(so * 32, 32)
    wrecv[pl.ds(own, 32)] = wsend[pl.ds(own, 32)]
    wall_arrivals()
    for o in range(N_SOLID):
        for layer in range(2):
            for i, part in enumerate(split(wrecv[o * 32 + layer * 16 : o * 32 + layer * 16 + 16, :])):
                at = (layer * 2 + i) * 32 + (o & 1) * 16
                wl[at : at + 16, (o >> 1) * 128 : (o >> 1) * 128 + 128] = part

    def wall_chunk(n, _):
        cols = oh_slot[:, pl.ds(pl.multiple_of(n * 512, 512), 512)]
        found = dot(wl[...], cols)
        for j in range(4):
            at = n * 4 + j
            mask = iota((32, 128), 0) == rslot[pl.ds(at, 1), :]
            part = found[:, j * 128 : (j + 1) * 128]
            for ref, base in ((t_face, 0), (i_face, 64)):
                both = part[base : base + 32] + part[base + 32 : base + 64]
                ref[pl.ds(at, 1), :] = jnp.sum(jnp.where(mask, both, 0.0), axis=0, keepdims=True)
        return 0

    lax.fori_loop(0, FACES // 512, wall_chunk, 0, unroll=4)
    t0 = t_face[...]
    t1 = i_face[...]
    between = 0.5 * (jnp.exp(CONDUCT_SLOPE * t0) + jnp.exp(CONDUCT_SLOPE * t1)) * (t1 - t0)
    i_face[...] = between

    def halves(x):
        high, low = split(x)
        return high.astype(F32), low.astype(F32)

    fields = halves(t0) + halves(between)
    for j in range(ROWS):
        cols = slice(j * 128, (j + 1) * 128)
        marks = vm[0:128, cols]
        for i, field in enumerate(fields):
            vm[(i + 1) * 128 : (i + 2) * 128, cols] = marks * wide(field[j : j + 1, :], 8)
    sums = dot_t(vm[...], oh_cell[...])
    for part in range(4):
        cols, rows = slice(part * 128, (part + 1) * 128), slice(part * 128, (part + 1) * 128)
        count[rows, :] = sums[0:128, cols]
        s_sum[rows, :] = sums[128:256, cols] + sums[256:384, cols]
        i_sum[rows, :] = sums[384:512, cols] + sums[512:640, cols]

    precursor_arrivals()
    window = jnp.concatenate(
        [
            jnp.concatenate(
                [win[step, 0:4].reshape(256, 128), win[step, 4:8].reshape(256, 128)], axis=1
            )
            for step in range(2)
        ],
        axis=0,
    )
    for g in range(CY // 4):
        found = dot(window, oh_in[:, g * 512 : (g + 1) * 512])
        for j in range(4):
            y = g * 4 + j
            mask = iota((64, 128), 0) == ri[y : y + 1, :]
            for step, dst in ((0, q0), (1, q1)):
                part = found[step * 256 : (step + 1) * 256, j * 128 : (j + 1) * 128]
                for c in range(NV):
                    total = None
                    for src in range(4):
                        term = jnp.where(
                            mask[src * 16 : src * 16 + 16],
                            part[src * 64 + c * 16 : src * 64 + c * 16 + 16],
                            0.0,
                        )
                        total = term if total is None else total + term
                    dst[c, 0, TOP + y : TOP + y + 1, :] = jnp.sum(total, axis=0, keepdims=True)

    def receive_halos(step, copies, dst):
        for copy in copies:
            copy.wait_recv()

        def rows_of(x, _):
            for c in range(NV):
                k = c * XL + x
                dst[c, x + 1, TOP - 1 : TOP, :] = jnp.where(
                    fl > 0, hy_recv[step, 0, pl.ds(k, 1), :], 0.0
                )
                dst[c, x + 1, TOP + CY : TOP + CY + 1, :] = jnp.where(
                    fl < N_FLUID - 1, hy_recv[step, 1, pl.ds(k, 1), :], 0.0
                )
            return 0

        lax.fori_loop(0, XL, rows_of, 0, unroll=8)
        merged = []
        for part in range(2):
            low = jnp.where(inf > 0, pltpu.roll(hz_recv[step, 0, part], 1, 1), 0.0)
            high = jnp.where(inf < N_INFLOW - 1, pltpu.roll(hz_recv[step, 1, part], 127, 1), 0.0)
            merged.append(jnp.where((lane & 1) == 1, low, high))
        return merged

    first_lane, last_lane = lane == 0, lane == CZ - 1

    def advanced(src, merged, x):
        centre = [src[c, x + 1, TOP : TOP + CY, :] for c in range(NV)]
        half = 0.5 * TIME_STEP
        slopes = [half * speed for speed in centre[:3]]
        ahead = [VISCOSITY * TIME_STEP - slope for slope in slopes]
        behind = [VISCOSITY * TIME_STEP + slope for slope in slopes]
        fresh = []
        for c in range(NV):
            q = centre[c]
            j = pair_of(c, x)
            edge = pltpu.roll(merged[c // 2], 127 - 2 * j, 1)
            zm = jnp.where(first_lane, edge, pltpu.roll(q, 1, 1))
            zp = jnp.where(last_lane, edge, pltpu.roll(q, CZ - 1, 1))
            xm = src[c, x, TOP : TOP + CY, :]
            xp = src[c, x + 2, TOP : TOP + CY, :]
            ym = src[c, x + 1, TOP - 1 : TOP + CY - 1, :]
            yp = src[c, x + 1, TOP + 1 : TOP + CY + 1, :]
            along_x = ahead[0] * xp + behind[0] * xm
            along_y = ahead[1] * yp + behind[1] * ym
            along_z = ahead[2] * zp + behind[2] * zm
            fresh.append(
                (1.0 - 6.0 * VISCOSITY * TIME_STEP) * q + ((along_x + along_y) + along_z)
            )
        return centre, fresh

    merged_0 = receive_halos(0, halos_0, q0)

    def first(x, packed):
        rows = pl.ds(pl.multiple_of(x * CY, CY), CY)
        centre, fresh = advanced(q0, merged_0, x)
        u, v, w, temp = centre
        colder = s_sum[rows, :]
        total = transfer_of(u, v, w) * (count[rows, :] * temp - colder)
        i_sum[rows, :] = colder + SOLID_STEP * (i_sum[rows, :] + total)
        fresh[3] = fresh[3] - WALL_WEIGHT * total
        for c in range(NV):
            q1[c, x + 1, TOP : TOP + CY, :] = fresh[c]
        keep_sample_plane(x, *fresh)
        return keep_edges(1, x, fresh, packed)

    flux_0 = a_face[...] * (b_face[...] - t_face[...])
    packed = lax.fori_loop(0, XL, first, (zero_plane, zero_plane), unroll=2)
    hz_send[1, 0] = packed[0]
    hz_send[1, 1] = packed[1]
    halos_1 = halo_copies(1)
    for copy in halos_1:
        copy.start()
    for c in range(NV):
        q1[c, XL + 1, TOP : TOP + CY, :] = q1[c, XL, TOP : TOP + CY, :]

    sample_faces()
    t_later = t_face[...] + SOLID_STEP * (i_face[...] + flux_0)
    flux_1 = a_face[...] * (b_face[...] - t_later)
    parts = halves(flux_0) + halves(flux_1)
    for j in range(ROWS):
        cols = slice(j * 128, (j + 1) * 128)
        marks = oh_srow[:, cols]
        for i, part in enumerate(parts):
            vm[i * 32 : (i + 1) * 32, cols] = marks * wide(part[j : j + 1, :], 2)
    found = dot_t(vm[0:128, :], oh_slot[...])
    for step in range(2):
        both = found[step * 64 : step * 64 + 32] + found[step * 64 + 32 : step * 64 + 64]
        for o in range(N_SOLID):
            fsend[step, o * 16 : (o + 1) * 16] = both[
                (o & 1) * 16 : (o & 1) * 16 + 16, (o >> 1) * 128 : (o >> 1) * 128 + 128
            ]
    for copy in flux_copies:
        copy.start()
    own = pl.multiple_of(so * 16, 16)
    for step in range(2):
        frecv[step, pl.ds(own, 16)] = fsend[step, pl.ds(own, 16)]

    merged_1 = receive_halos(1, halos_1, q1)
    outs = []

    def second(x, _):
        rows = pl.ds(pl.multiple_of(x * CY, CY), CY)
        centre, fresh = advanced(q1, merged_1, x)
        u, v, w, temp = centre
        total = transfer_of(u, v, w) * (count[rows, :] * temp - i_sum[rows, :])
        fresh[3] = fresh[3] - WALL_WEIGHT * total
        for c in range(NV):
            ob[c, x] = fresh[c]
        return 0

    def second_half(part):
        lax.fori_loop(part * 16, part * 16 + 16, second, 0, unroll=2)
        out = pltpu.make_async_copy(
            ob.at[:, pl.ds(part * 16, 16)],
            out_state.at[:, pl.ds(part * 16, 16)],
            out_sem.at[part],
        )
        out.start()
        outs.append(out)

    second_half(0)

    layer = iota((LAYERS, 128), 0)

    def conduct(temps, flux_row):
        conductivity = jnp.exp(CONDUCT_SLOPE * temps)
        above = pltpu.roll(temps, LAYERS - 1, 0)
        c_above = pltpu.roll(conductivity, LAYERS - 1, 0)
        flow = jnp.where(
            layer == LAYERS - 1,
            conductivity * (0.0 - temps),
            0.5 * (conductivity + c_above) * (above - temps),
        )
        from_below = jnp.where(layer == 0, flux_row, -pltpu.roll(flow, 1, 0))
        return temps + SOLID_STEP * (flow + from_below)

    flux_arrivals()

    def wall_tiles(t, _):
        cols = [pl.ds(pl.multiple_of((t * 8 + i) * 128, 128), 128) for i in range(8)]
        temps = [wv[:, col] for col in cols]
        for step in range(2):
            rows = [frecv[step, pl.ds(t * 8 + i, 1), :] for i in range(8)]
            temps = [conduct(temp, flux_row) for temp, flux_row in zip(temps, rows)]
        for col, temp in zip(cols, temps):
            wv[:, col] = temp
        return 0

    lax.fori_loop(0, COLUMNS // 1024, wall_tiles, 0)
    out = pltpu.make_async_copy(wv, out_wall, out_sem.at[2])
    out.start()
    outs.append(out)

    second_half(1)
    for copy in wall_copies + precursor_copies + halos_0 + halos_1 + flux_copies:
        copy.wait_send()
    for out in outs:
        out.wait()


def local(state, precursor, inlet_map, face_cell, face_owner, wall_temp):
    any_space = pl.BlockSpec(memory_space=pl.ANY)
    vmem = pltpu.VMEM
    dma = pltpu.SemaphoreType.DMA
    new_state, new_wall = pl.pallas_call(
        kernel,
        out_shape=(
            jax.ShapeDtypeStruct((NV, XL, CY, CZ), F32),
            jax.ShapeDtypeStruct((LAYERS, COLUMNS), F32),
        ),
        in_specs=[any_space] * 6,
        out_specs=(any_space, any_space),
        scratch_shapes=[
            vmem((NV, XL + 2, PITCH, CZ), F32),
            vmem((NV, XL + 2, PITCH, CZ), F32),
            vmem((NV, XL, CY, CZ), F32),
            vmem((LAYERS, COLUMNS), F32),
            vmem((2, NV, CAP), BF16),
            vmem((CY, CZ), I32),
            vmem((ROWS, 128), I32),
            vmem((ROWS, 128), I32),
            vmem((2, 64, 128), F32),
            vmem((2, N_INFLOW, 64, 128), BF16),
            vmem((128, 128), F32),
            vmem((128, 128), F32),
            vmem((2, 2, 128, 128), F32),
            vmem((2, 2, 128, 128), F32),
            vmem((2, 2, CY, 128), F32),
            vmem((2, 2, 2, CY, 128), F32),
            vmem((2, 64, 128), F32),
            vmem((2, 64, 128), F32),
            vmem((512, FACES), BF16),
            vmem((256, FACES), BF16),
            vmem((256, CY * CZ), BF16),
            vmem((32, FACES), BF16),
            vmem((640, FACES), BF16),
            vmem((4, 512, 128), BF16),
            vmem((128, 256), BF16),
            vmem((ROWS, 128), F32),
            vmem((ROWS, 128), F32),
            vmem((ROWS, 128), F32),
            vmem((ROWS, 128), F32),
            vmem((ROWS, 128), F32),
            vmem((ROWS, 128), F32),
            vmem((CY, 128), F32),
            vmem((CY, 128), F32),
            vmem((CY, 128), I32),
            vmem((ROWS, 128), I32),
            vmem((ROWS, 128), I32),
            vmem((512, 128), F32),
            vmem((512, 128), F32),
            vmem((512, 128), F32),
            vmem((ROWS, 128), F32),
            vmem((ROWS, 128), F32),
            vmem((ROWS, 128), F32),
            vmem((ROWS, 128), F32),
            dma((6,)),
            dma((N_INFLOW - 1,)),
            dma((N_INFLOW - 1,)),
            dma((N_SOLID - 1,)),
            dma((N_SOLID - 1,)),
            dma((2, 2, 2)),
            dma((2, 2, 2)),
            dma((N_SOLID - 1,)),
            dma((N_SOLID - 1,)),
            dma((3,)),
        ],
        compiler_params=pltpu.CompilerParams(
            collective_id=0, has_side_effects=True, vmem_limit_bytes=62 * 1024 * 1024
        ),
        name="manifold_step",
    )(
        state[0],
        precursor[0],
        inlet_map[0],
        face_cell.reshape(ROWS, 128),
        face_owner.reshape(ROWS, 128),
        wall_temp[0, 0, 0],
    )
    return new_state[None], new_wall[None, None, None]


def solution(mesh):
    return jax.shard_map(
        local,
        mesh=mesh,
        in_specs=(
            P("solid", None, None, "fluid", "inflow"),
            P("solid", None, None, ("fluid", "inflow")),
            P("solid", "fluid", "inflow"),
            P("solid", "fluid", "inflow", None),
            P("solid", "fluid", "inflow", None, None),
            P("solid", "fluid", "inflow", None, None),
        ),
        out_specs=(
            P("solid", None, None, "fluid", "inflow"),
            P("solid", "fluid", "inflow", None, None),
        ),
        check_vma=False,
    )
```

```python
import functools

import jax
import jax.numpy as jnp
from jax import lax
from jax.experimental import pallas as pl
from jax.experimental.pallas import tpu as pltpu
from jax.sharding import PartitionSpec as P

F32, BF16, I32 = jnp.float32, jnp.bfloat16, jnp.int32
MESH = pl.DeviceIdType.MESH

XL, CY, CZ, NV = 32, 16, 128, 4
CAP, LAYERS, FACES = 2048, 8, 4096
N_FLUID, N_INFLOW, N_SOLID = 8, 8, 4
COLUMNS = N_SOLID * CAP
ROWS = FACES // 128
TOP, PITCH = 8, 32
CHUNK = 512
CHUNKS = FACES // CHUNK
PLANES = XL // CHUNKS

TIME_STEP = 0.1
VISCOSITY = 0.5
HEAT_TRANSFER = 0.8
CONDUCT_SLOPE = 0.2
SOLID_STEP = 0.15
WALL_WEIGHT = 0.5


def split(x):
    high = x.astype(BF16)
    return high, (x - high.astype(F32)).astype(BF16)


def transfer_of(u, v, w):
    return HEAT_TRANSFER * (1.0 + 0.5 * (u * u + v * v + w * w))


def iota(shape, dim):
    return lax.broadcasted_iota(I32, shape, dim)


def bits(mask):
    return jnp.where(mask, 1.0, 0.0).astype(BF16)


def dot(a, b):
    return lax.dot_general(a, b, (((1,), (0,)), ((), ())), preferred_element_type=F32)


def dot_t(a, b):
    return lax.dot_general(a, b, (((1,), (1,)), ((), ())), preferred_element_type=F32)


def kernel(
    state,
    prec,
    imap,
    fcell,
    fown,
    wall,
    out_state,
    out_flux,
    q0,
    q1,
    wv,
    pv,
    imv,
    fcv,
    fov,
    psend,
    win,
    wsend,
    wrecv,
    hy_send,
    hy_recv,
    hz_send,
    hz_recv,
    fsend,
    frecv,
    oh_cell,
    oh_slot,
    oh_in,
    oh_srow,
    vm,
    fm,
    lhs_0,
    lhs_1,
    wl,
    zf,
    qf,
    rf,
    lf,
    hf,
    sf,
    zi,
    hi_in,
    ri,
    rcell,
    rslot,
    count,
    s_sum,
    f_sum,
    later,
    a_face,
    b_face,
    t_face,
    i_face,
    f_face,
    found_0,
    found_1,
    load_sem,
    p_send_sem,
    p_recv_sem,
    w_send_sem,
    w_recv_sem,
    h_send_sem,
    h_recv_sem,
    f_send_sem,
    f_recv_sem,
):
    fl, inf, so = lax.axis_index("fluid"), lax.axis_index("inflow"), lax.axis_index("solid")

    loads = [
        pltpu.make_async_copy(prec, pv, load_sem.at[0]),
        pltpu.make_async_copy(wall, wv, load_sem.at[1]),
        pltpu.make_async_copy(fown, fov, load_sem.at[3]),
        pltpu.make_async_copy(fcell, fcv, load_sem.at[4]),
        pltpu.make_async_copy(imap, imv, load_sem.at[5]),
        pltpu.make_async_copy(state, q0.at[:, pl.ds(1, XL), pl.ds(TOP, CY)], load_sem.at[2]),
    ]
    for load in loads:
        load.start()

    barrier = pltpu.get_barrier_semaphore()

    def greet(ids):
        pl.semaphore_signal(barrier, inc=1, device_id=ids, device_id_type=MESH)

    for d in range(1, N_INFLOW):
        greet({"inflow": (inf + d) & (N_INFLOW - 1)})
    for d in (1, N_FLUID - 1):
        greet({"fluid": (fl + d) & (N_FLUID - 1)})
    for d in range(1, N_SOLID):
        greet({"solid": (so + d) & (N_SOLID - 1)})

    lane = iota((CY, CZ), 1)

    loads[0].wait()
    for s in range(2):
        for k in range(16):
            psend[s, pl.ds(k, 4, stride=16), :] = pv[s, :, k * 128 : (k + 1) * 128].astype(F32)
    for s in range(2):
        win[s, inf] = psend[s].astype(BF16)
    loads[1].wait()
    for t in range(64):
        wsend[pl.ds(t // 16 * 32 + t % 16, 2, stride=16), :] = wv[0:2, t * 128 : (t + 1) * 128]

    wall_copies = []
    for d in range(1, N_SOLID):
        to = (so + d) & (N_SOLID - 1)
        wall_copies.append(
            pltpu.make_async_remote_copy(
                src_ref=wsend.at[pl.ds(pl.multiple_of(to * 32, 32), 32)],
                dst_ref=wrecv.at[pl.ds(pl.multiple_of(so * 32, 32), 32)],
                send_sem=w_send_sem.at[d - 1],
                recv_sem=w_recv_sem.at[d - 1],
                device_id={"solid": to},
                device_id_type=MESH,
            )
        )

    def halo_copies(step):
        copies = []
        for side in range(2):
            far = N_FLUID - 1 if side == 0 else 1
            copies.append(
                pltpu.make_async_remote_copy(
                    src_ref=hy_send.at[step, side],
                    dst_ref=hy_recv.at[step, 1 - side],
                    send_sem=h_send_sem.at[step, 0, side],
                    recv_sem=h_recv_sem.at[step, 0, side],
                    device_id={"fluid": (fl + far) & (N_FLUID - 1)},
                    device_id_type=MESH,
                )
            )
        for side in range(2):
            far = N_INFLOW - 1 if side == 0 else 1
            copies.append(
                pltpu.make_async_remote_copy(
                    src_ref=hz_send.at[step],
                    dst_ref=hz_recv.at[step, 1 - side],
                    send_sem=h_send_sem.at[step, 1, side],
                    recv_sem=h_recv_sem.at[step, 1, side],
                    device_id={"inflow": (inf + far) & (N_INFLOW - 1)},
                    device_id_type=MESH,
                )
            )
        return copies

    precursor_copies = [
        pltpu.make_async_remote_copy(
            src_ref=win.at[:, inf],
            dst_ref=win.at[:, inf],
            send_sem=p_send_sem.at[d - 1],
            recv_sem=p_recv_sem.at[d - 1],
            device_id={"inflow": (inf + d) & (N_INFLOW - 1)},
            device_id_type=MESH,
        )
        for d in range(1, N_INFLOW)
    ]

    def precursor_arrivals():
        for d in range(1, N_INFLOW):
            came = (inf + N_INFLOW - d) & (N_INFLOW - 1)
            pltpu.make_async_remote_copy(
                src_ref=win.at[:, came],
                dst_ref=win.at[:, came],
                send_sem=p_send_sem.at[d - 1],
                recv_sem=p_recv_sem.at[d - 1],
                device_id={"inflow": came},
                device_id_type=MESH,
            ).wait_recv()

    def wall_arrivals():
        for d in range(1, N_SOLID):
            came = (so + N_SOLID - d) & (N_SOLID - 1)
            pltpu.make_async_remote_copy(
                src_ref=wsend.at[pl.ds(pl.multiple_of(came * 32, 32), 32)],
                dst_ref=wrecv.at[pl.ds(pl.multiple_of(came * 32, 32), 32)],
                send_sem=w_send_sem.at[d - 1],
                recv_sem=w_recv_sem.at[d - 1],
                device_id={"solid": came},
                device_id_type=MESH,
            ).wait_recv()

    def flux_arrivals():
        for d in range(1, N_SOLID):
            came = (so + N_SOLID - d) & (N_SOLID - 1)
            pltpu.make_async_remote_copy(
                src_ref=fsend.at[:, pl.ds(pl.multiple_of(came * 16, 16), 16)],
                dst_ref=frecv.at[:, pl.ds(pl.multiple_of(came * 16, 16), 16)],
                send_sem=f_send_sem.at[d - 1],
                recv_sem=f_recv_sem.at[d - 1],
                device_id={"solid": came},
                device_id_type=MESH,
            ).wait_recv()

    pl.semaphore_wait(barrier, (N_INFLOW - 1) + 2 + (N_SOLID - 1))
    for copy in wall_copies + precursor_copies:
        copy.start()

    def pair_of(c, x):
        return (c % 2) * XL + x

    def keep_edges(step, x, values, packed):
        packed = list(packed)
        for c in range(NV):
            k = c * XL + x
            hy_send[step, 0, pl.ds(k, 1), :] = values[c][0:1]
            hy_send[step, 1, pl.ds(k, 1), :] = values[c][CY - 1 : CY]
            j = pair_of(c, x)
            moved = pltpu.roll(values[c], 2 * j + 1, 1)
            packed[c // 2] = jnp.where(lax.shift_right_logical(lane, 1) == j, moved, packed[c // 2])
        return tuple(packed)

    zero_plane = jnp.zeros((CY, CZ), F32)
    lhs = (lhs_0, lhs_1)

    def keep_sample_plane(step, x, u, v, w, temp):
        (a_high, a_low), (b_high, b_low) = split(transfer_of(u, v, w)), split(temp)
        parts = (a_high, b_high, a_low, b_low)
        quarter = lax.shift_right_logical(x, 3)
        at = pl.multiple_of((x & 7) * CY, CY)
        for i, part in enumerate(parts):
            lhs[step][quarter, pl.ds(i * 128 + at, CY), :] = part

    for load in loads[2:5]:
        load.wait()
    cell = fcv[...]
    qf[...] = lax.shift_right_logical(cell, 14).astype(F32)
    zf[...] = (cell & 127).astype(F32)
    r = lax.shift_right_logical(cell, 7) & 127
    rcell[...] = r
    rf[...] = r.astype(F32)
    owner = fov[...]
    marks = jnp.concatenate([jnp.where(owner == o, 1.0, 0.0) for o in range(N_SOLID)], axis=0)
    upper = jnp.where(iota((128, 128), 0) < iota((128, 128), 1), 1.0, 0.0)
    earlier = dot(
        marks.astype(BF16), jnp.concatenate([upper, jnp.ones((128, 128), F32)], axis=1).astype(BF16)
    )
    r_out, r_in = iota((128, 128), 0), iota((128, 128), 1)
    same = lax.shift_right_logical(r_out, 5) == lax.shift_right_logical(r_in, 5)
    below = bits(jnp.logical_and(same, r_in < r_out))
    ranks = (earlier[:, :128] + dot(below, earlier[:, 128:].astype(BF16))) * marks
    rank = ranks[0:32] + ranks[32:64] + ranks[64:96] + ranks[96:128]
    slot = owner * CAP + rank.astype(I32)
    hi = lax.shift_right_logical(slot, 7)
    hf[...] = lax.shift_right_logical(hi, 5).astype(F32)
    lf[...] = (slot & 127).astype(F32)
    rslot[...] = hi & 31
    sf[...] = (hi & 31).astype(F32)
    relative = imv[...] - fl * (N_INFLOW * CAP)
    hi = lax.shift_right_logical(relative, 7)
    zi[...] = (relative & 127).astype(F32)
    hi_in[...] = lax.shift_right_logical(hi, 6).astype(F32)
    ri[...] = hi & 63

    steps_128 = iota((128, 128), 0).astype(F32).astype(BF16)
    one, zero = jnp.ones((), BF16), jnp.zeros((), BF16)

    def wide(row_values, blocks):
        tile = jnp.broadcast_to(row_values, (16, 128)).astype(BF16)
        return jnp.concatenate([tile] * blocks, axis=0) if blocks > 1 else tile

    def hot(row_values, blocks):
        return jnp.where(steps_128[: blocks * 16] == wide(row_values, blocks), one, zero)

    def marked(row_values, value, blocks):
        return wide(jnp.where(row_values == value, 1.0, 0.0), blocks)

    def lanes_of(j):
        return pl.ds(pl.multiple_of(j * 128, 128), 128)

    def one_hots_of_faces(j):
        at, cols = pl.ds(j, 1), lanes_of(j)
        base, quarter = hot(zf[at, :], 8), qf[at, :]
        for part in range(4):
            oh_cell[part * 128 : (part + 1) * 128, cols] = base * marked(quarter, float(part), 8)
        vm[0:128, cols] = hot(rf[at, :], 8)
        base, half = hot(lf[at, :], 8), hf[at, :]
        for part in range(2):
            oh_slot[part * 128 : (part + 1) * 128, cols] = base * marked(half, float(part), 8)
        oh_srow[:, cols] = hot(sf[at, :], 2)

    def one_hots_of_inlet(j):
        at, cols = pl.ds(j, 1), lanes_of(j)
        base, half = hot(zi[at, :], 8), hi_in[at, :]
        for part in range(2):
            oh_in[part * 128 : (part + 1) * 128, cols] = base * marked(half, float(part), 8)

    loads[5].wait()

    def prepare(n, packed):
        for i in range(4):
            x = n * 4 + i
            values = [q0[c, x + 1, TOP : TOP + CY, :] for c in range(NV)]
            keep_sample_plane(0, x, *values)
            packed = keep_edges(0, x, values, packed)
            one_hots_of_faces(n * 4 + i)
        for i in range(2):
            one_hots_of_inlet(n * 2 + i)
        return packed

    packed = lax.fori_loop(0, XL // 4, prepare, (zero_plane, zero_plane))
    hz_send[0, 0] = packed[0]
    hz_send[0, 1] = packed[1]
    halos_0 = halo_copies(0)
    for copy in halos_0:
        copy.start()
    for c in range(NV):
        q0[c, XL + 1, TOP : TOP + CY, :] = q0[c, XL, TOP : TOP + CY, :]

    def sample_product(step, n, found):
        cols = oh_cell[:, pl.ds(pl.multiple_of(n * CHUNK, CHUNK), CHUNK)]
        fields = jnp.concatenate([lhs[step][i] for i in range(4)], axis=1)
        both = dot(fields, cols)
        found[...] = both[0:256] + both[256:512]

    def sample_pick(n, found):
        for j in range(CHUNK // 128):
            at = n * (CHUNK // 128) + j
            cols = slice(j * 128, (j + 1) * 128)
            mask = iota((128, 128), 0) == rcell[pl.ds(at, 1), :]
            for ref, base in ((a_face, 0), (b_face, 128)):
                both = found[base : base + 128, cols]
                ref[pl.ds(at, 1), :] = jnp.sum(jnp.where(mask, both, 0.0), axis=0, keepdims=True)

    def sample_faces(step, beside, carry):
        sample_product(step, 0, found_0)

        def two(m, carry):
            sample_product(step, 2 * m + 1, found_1)
            carry = beside(2 * m, carry)
            sample_pick(2 * m, found_0)
            sample_product(step, (2 * m + 2) & (CHUNKS - 1), found_0)
            carry = beside(2 * m + 1, carry)
            sample_pick(2 * m + 1, found_1)
            return carry

        return lax.fori_loop(0, CHUNKS // 2, two, carry)

    own = pl.multiple_of(so * 32, 32)
    wrecv[pl.ds(own, 32)] = wsend[pl.ds(own, 32)]
    wall_arrivals()
    for o in range(N_SOLID):
        for layer in range(2):
            for i, part in enumerate(split(wrecv[o * 32 + layer * 16 : o * 32 + layer * 16 + 16, :])):
                at = (layer * 2 + i) * 32 + (o & 1) * 16
                wl[at : at + 16, (o >> 1) * 128 : (o >> 1) * 128 + 128] = part

    for n in range(FACES // 512):
        found = dot(wl[...], oh_slot[:, n * 512 : (n + 1) * 512])
        for j in range(4):
            at = n * 4 + j
            mask = iota((32, 128), 0) == rslot[at : at + 1, :]
            part = found[:, j * 128 : (j + 1) * 128]
            for ref, base in ((t_face, 0), (i_face, 64)):
                both = part[base : base + 32] + part[base + 32 : base + 64]
                ref[at : at + 1, :] = jnp.sum(jnp.where(mask, both, 0.0), axis=0, keepdims=True)
    t0 = t_face[...]
    t1 = i_face[...]
    between = 0.5 * (jnp.exp(CONDUCT_SLOPE * t0) + jnp.exp(CONDUCT_SLOPE * t1)) * (t1 - t0)
    i_face[...] = between

    def halves(x):
        high, low = split(x)
        return high.astype(F32), low.astype(F32)

    fields = halves(t0) + halves(between)
    for j in range(ROWS):
        cols = slice(j * 128, (j + 1) * 128)
        marks = vm[0:128, cols]
        for i, field in enumerate(fields):
            vm[(i + 1) * 128 : (i + 2) * 128, cols] = marks * wide(field[j : j + 1, :], 8)
    sums = dot_t(vm[...], oh_cell[...])
    for part in range(4):
        cols, rows = slice(part * 128, (part + 1) * 128), slice(part * 128, (part + 1) * 128)
        count[rows, :] = sums[0:128, cols]
        s_sum[rows, :] = sums[128:256, cols] + sums[256:384, cols]
        f_sum[rows, :] = sums[384:512, cols] + sums[512:640, cols]

    precursor_arrivals()
    window = jnp.concatenate(
        [
            jnp.concatenate(
                [win[step, 0:4].reshape(256, 128), win[step, 4:8].reshape(256, 128)], axis=1
            )
            for step in range(2)
        ],
        axis=0,
    )
    for g in range(CY // 4):
        found = dot(window, oh_in[:, g * 512 : (g + 1) * 512])
        for j in range(4):
            y = g * 4 + j
            mask = iota((64, 128), 0) == ri[y : y + 1, :]
            for step, dst in ((0, q0), (1, q1)):
                part = found[step * 256 : (step + 1) * 256, j * 128 : (j + 1) * 128]
                for c in range(NV):
                    total = None
                    for src in range(4):
                        term = jnp.where(
                            mask[src * 16 : src * 16 + 16],
                            part[src * 64 + c * 16 : src * 64 + c * 16 + 16],
                            0.0,
                        )
                        total = term if total is None else total + term
                    dst[c, 0, TOP + y : TOP + y + 1, :] = jnp.sum(total, axis=0, keepdims=True)

    def receive_halos(step, copies, dst):
        for copy in copies:
            copy.wait_recv()

        def rows_of(x, _):
            for c in range(NV):
                k = c * XL + x
                dst[c, x + 1, TOP - 1 : TOP, :] = jnp.where(
                    fl > 0, hy_recv[step, 0, pl.ds(k, 1), :], 0.0
                )
                dst[c, x + 1, TOP + CY : TOP + CY + 1, :] = jnp.where(
                    fl < N_FLUID - 1, hy_recv[step, 1, pl.ds(k, 1), :], 0.0
                )
            return 0

        lax.fori_loop(0, XL, rows_of, 0, unroll=8)
        merged = []
        for part in range(2):
            low = jnp.where(inf > 0, pltpu.roll(hz_recv[step, 0, part], 1, 1), 0.0)
            high = jnp.where(inf < N_INFLOW - 1, pltpu.roll(hz_recv[step, 1, part], 127, 1), 0.0)
            merged.append(jnp.where((lane & 1) == 1, low, high))
        return merged

    first_lane, last_lane = lane == 0, lane == CZ - 1

    def advanced(src, merged, x):
        centre = [src[c, x + 1, TOP : TOP + CY, :] for c in range(NV)]
        half = 0.5 * TIME_STEP
        slopes = [half * speed for speed in centre[:3]]
        ahead = [VISCOSITY * TIME_STEP - slope for slope in slopes]
        behind = [VISCOSITY * TIME_STEP + slope for slope in slopes]
        fresh = []
        for c in range(NV):
            q = centre[c]
            j = pair_of(c, x)
            edge = pltpu.roll(merged[c // 2], 127 - 2 * j, 1)
            zm = jnp.where(first_lane, edge, pltpu.roll(q, 1, 1))
            zp = jnp.where(last_lane, edge, pltpu.roll(q, CZ - 1, 1))
            xm = src[c, x, TOP : TOP + CY, :]
            xp = src[c, x + 2, TOP : TOP + CY, :]
            ym = src[c, x + 1, TOP - 1 : TOP + CY - 1, :]
            yp = src[c, x + 1, TOP + 1 : TOP + CY + 1, :]
            along_x = ahead[0] * xp + behind[0] * xm
            along_y = ahead[1] * yp + behind[1] * ym
            along_z = ahead[2] * zp + behind[2] * zm
            fresh.append(
                (1.0 - 6.0 * VISCOSITY * TIME_STEP) * q + ((along_x + along_y) + along_z)
            )
        return centre, fresh

    merged_0 = receive_halos(0, halos_0, q0)

    def first(n, packed):
        for i in range(PLANES):
            x = n * PLANES + i
            rows = pl.ds(pl.multiple_of(x * CY, CY), CY)
            centre, fresh = advanced(q0, merged_0, x)
            u, v, w, temp = centre
            colder = s_sum[rows, :]
            total = transfer_of(u, v, w) * (count[rows, :] * temp - colder)
            later[rows, :] = colder + SOLID_STEP * (f_sum[rows, :] + total)
            fresh[3] = fresh[3] - WALL_WEIGHT * total
            for c in range(NV):
                q1[c, x + 1, TOP : TOP + CY, :] = fresh[c]
            keep_sample_plane(1, x, *fresh)
            packed = keep_edges(1, x, fresh, packed)
        return packed

    packed = sample_faces(0, first, (zero_plane, zero_plane))
    hz_send[1, 0] = packed[0]
    hz_send[1, 1] = packed[1]
    halos_1 = halo_copies(1)
    for copy in halos_1:
        copy.start()
    for c in range(NV):
        q1[c, XL + 1, TOP : TOP + CY, :] = q1[c, XL, TOP : TOP + CY, :]

    flux_0 = a_face[...] * (b_face[...] - t_face[...])
    t_face[...] = t_face[...] + SOLID_STEP * (i_face[...] + flux_0)
    f_face[...] = flux_0
    sample_faces(1, lambda n, carry: carry, 0)
    parts = halves(f_face[...]) + halves(a_face[...] * (b_face[...] - t_face[...]))
    for j in range(ROWS):
        cols = slice(j * 128, (j + 1) * 128)
        marks = oh_srow[:, cols]
        for i, part in enumerate(parts):
            fm[i * 32 : (i + 1) * 32, cols] = marks * wide(part[j : j + 1, :], 2)
    found = jnp.transpose(dot_t(oh_slot[...], fm[...]))
    for step in range(2):
        both = found[step * 64 : step * 64 + 32] + found[step * 64 + 32 : step * 64 + 64]
        for o in range(N_SOLID):
            fsend[step, o * 16 : (o + 1) * 16] = both[
                (o & 1) * 16 : (o & 1) * 16 + 16, (o >> 1) * 128 : (o >> 1) * 128 + 128
            ]
    flux_copies = []
    for d in range(1, N_SOLID):
        to = (so + d) & (N_SOLID - 1)
        flux_copies.append(
            pltpu.make_async_remote_copy(
                src_ref=fsend.at[:, pl.ds(pl.multiple_of(to * 16, 16), 16)],
                dst_ref=frecv.at[:, pl.ds(pl.multiple_of(so * 16, 16), 16)],
                send_sem=f_send_sem.at[d - 1],
                recv_sem=f_recv_sem.at[d - 1],
                device_id={"solid": to},
                device_id_type=MESH,
            )
        )
    for copy in flux_copies:
        copy.start()
    own = pl.multiple_of(so * 16, 16)
    for step in range(2):
        frecv[step, pl.ds(own, 16)] = fsend[step, pl.ds(own, 16)]

    merged_1 = receive_halos(1, halos_1, q1)

    def second(x, _):
        rows = pl.ds(pl.multiple_of(x * CY, CY), CY)
        centre, fresh = advanced(q1, merged_1, x)
        u, v, w, temp = centre
        total = transfer_of(u, v, w) * (count[rows, :] * temp - later[rows, :])
        fresh[3] = fresh[3] - WALL_WEIGHT * total
        for c in range(NV):
            out_state[c, x] = fresh[c]
        return 0

    lax.fori_loop(0, XL, second, 0, unroll=4)
    flux_arrivals()
    out_flux[...] = frecv[...]
    for copy in wall_copies + precursor_copies + halos_0 + halos_1 + flux_copies:
        copy.wait_send()


def finish(fluid, flux, wall, out_state, out_wall, wv, fv, load_sem, out_sem):
    loads = [
        pltpu.make_async_copy(flux, fv, load_sem.at[0]),
        pltpu.make_async_copy(wall, wv, load_sem.at[1]),
    ]
    outs = [pltpu.make_async_copy(fluid.at[c], out_state.at[c], out_sem.at[c]) for c in range(NV)]
    for copy in loads + outs:
        copy.start()
    for load in loads:
        load.wait()
    layer = iota((LAYERS, 128), 0)

    def conduct(temps, flux_row):
        conductivity = jnp.exp(CONDUCT_SLOPE * temps)
        above = pltpu.roll(temps, LAYERS - 1, 0)
        c_above = pltpu.roll(conductivity, LAYERS - 1, 0)
        flow = jnp.where(
            layer == LAYERS - 1,
            conductivity * (0.0 - temps),
            0.5 * (conductivity + c_above) * (above - temps),
        )
        from_below = jnp.where(layer == 0, flux_row, -pltpu.roll(flow, 1, 0))
        return temps + SOLID_STEP * (flow + from_below)

    def wall_tiles(t, _):
        cols = [pl.ds(pl.multiple_of((t * 16 + i) * 128, 128), 128) for i in range(16)]
        temps = [wv[:, col] for col in cols]
        for step in range(2):
            rows = [fv[step, pl.ds(t * 16 + i, 1), :] for i in range(16)]
            temps = [conduct(temp, flux_row) for temp, flux_row in zip(temps, rows)]
        for col, temp in zip(cols, temps):
            wv[:, col] = temp
        return 0

    lax.fori_loop(0, COLUMNS // 2048, wall_tiles, 0)
    out = pltpu.make_async_copy(wv, out_wall, out_sem.at[4])
    out.start()
    for copy in outs + [out]:
        copy.wait()


def local(state, precursor, inlet_map, face_cell, face_owner, wall_temp):
    any_space = pl.BlockSpec(memory_space=pl.ANY)
    vmem = pltpu.VMEM
    dma = pltpu.SemaphoreType.DMA
    fluid, flux = pl.pallas_call(
        kernel,
        out_shape=(vmem((NV, XL, CY, CZ), F32), vmem((2, 64, 128), F32)),
        in_specs=[any_space] * 6,
        out_specs=(pl.BlockSpec(memory_space=vmem),) * 2,
        scratch_shapes=[
            vmem((NV, XL + 2, PITCH, CZ), F32),
            vmem((NV, XL + 2, PITCH, CZ), F32),
            vmem((LAYERS, COLUMNS), F32),
            vmem((2, NV, CAP), BF16),
            vmem((CY, CZ), I32),
            vmem((ROWS, 128), I32),
            vmem((ROWS, 128), I32),
            vmem((2, 64, 128), F32),
            vmem((2, N_INFLOW, 64, 128), BF16),
            vmem((128, 128), F32),
            vmem((128, 128), F32),
            vmem((2, 2, 128, 128), F32),
            vmem((2, 2, 128, 128), F32),
            vmem((2, 2, CY, 128), F32),
            vmem((2, 2, 2, CY, 128), F32),
            vmem((2, 64, 128), F32),
            vmem((2, 64, 128), F32),
            vmem((512, FACES), BF16),
            vmem((256, FACES), BF16),
            vmem((256, CY * CZ), BF16),
            vmem((32, FACES), BF16),
            vmem((640, FACES), BF16),
            vmem((128, FACES), BF16),
            vmem((4, 512, 128), BF16),
            vmem((4, 512, 128), BF16),
            vmem((128, 256), BF16),
            vmem((ROWS, 128), F32),
            vmem((ROWS, 128), F32),
            vmem((ROWS, 128), F32),
            vmem((ROWS, 128), F32),
            vmem((ROWS, 128), F32),
            vmem((ROWS, 128), F32),
            vmem((CY, 128), F32),
            vmem((CY, 128), F32),
            vmem((CY, 128), I32),
            vmem((ROWS, 128), I32),
            vmem((ROWS, 128), I32),
            vmem((512, 128), F32),
            vmem((512, 128), F32),
            vmem((512, 128), F32),
            vmem((512, 128), F32),
            vmem((ROWS, 128), F32),
            vmem((ROWS, 128), F32),
            vmem((ROWS, 128), F32),
            vmem((ROWS, 128), F32),
            vmem((ROWS, 128), F32),
            vmem((256, CHUNK), F32),
            vmem((256, CHUNK), F32),
            dma((6,)),
            dma((N_INFLOW - 1,)),
            dma((N_INFLOW - 1,)),
            dma((N_SOLID - 1,)),
            dma((N_SOLID - 1,)),
            dma((2, 2, 2)),
            dma((2, 2, 2)),
            dma((N_SOLID - 1,)),
            dma((N_SOLID - 1,)),
        ],
        compiler_params=pltpu.CompilerParams(
            collective_id=0, has_side_effects=True, vmem_limit_bytes=60 * 1024 * 1024
        ),
        name="manifold_step",
    )(
        state[0],
        precursor[0],
        inlet_map[0],
        face_cell.reshape(ROWS, 128),
        face_owner.reshape(ROWS, 128),
        wall_temp[0, 0, 0],
    )
    new_state, new_wall = pl.pallas_call(
        finish,
        out_shape=(
            jax.ShapeDtypeStruct((NV, XL, CY, CZ), F32),
            jax.ShapeDtypeStruct((LAYERS, COLUMNS), F32),
        ),
        in_specs=[any_space] * 3,
        out_specs=(any_space, any_space),
        scratch_shapes=[
            vmem((LAYERS, COLUMNS), F32),
            vmem((2, 64, 128), F32),
            dma((2,)),
            dma((1 + NV,)),
        ],
        compiler_params=pltpu.CompilerParams(vmem_limit_bytes=8 * 1024 * 1024),
        name="finish",
    )(fluid, flux, wall_temp[0, 0, 0])
    return new_state[None], new_wall[None, None, None]


def solution(mesh):
    return jax.shard_map(
        local,
        mesh=mesh,
        in_specs=(
            P("solid", None, None, "fluid", "inflow"),
            P("solid", None, None, ("fluid", "inflow")),
            P("solid", "fluid", "inflow"),
            P("solid", "fluid", "inflow", None),
            P("solid", "fluid", "inflow", None, None),
            P("solid", "fluid", "inflow", None, None),
        ),
        out_specs=(
            P("solid", None, None, "fluid", "inflow"),
            P("solid", "fluid", "inflow", None, None),
        ),
        check_vma=False,
    )
```

```python
import functools

import jax
import jax.numpy as jnp
from jax import lax
from jax.experimental import pallas as pl
from jax.experimental.pallas import tpu as pltpu
from jax.sharding import PartitionSpec as P

F32, BF16, I32 = jnp.float32, jnp.bfloat16, jnp.int32
MESH = pl.DeviceIdType.MESH

XL, CY, CZ, NV = 32, 16, 128, 4
CAP, LAYERS, FACES = 2048, 8, 4096
N_FLUID, N_INFLOW, N_SOLID = 8, 8, 4
COLUMNS = N_SOLID * CAP
ROWS = FACES // 128
TOP, PITCH = 8, 32
CHUNK = 512
CHUNKS = FACES // CHUNK
PLANES = XL // CHUNKS

TIME_STEP = 0.1
VISCOSITY = 0.5
HEAT_TRANSFER = 0.8
CONDUCT_SLOPE = 0.2
SOLID_STEP = 0.15
WALL_WEIGHT = 0.5


def split(x):
    high = x.astype(BF16)
    return high, (x - high.astype(F32)).astype(BF16)


def transfer_of(u, v, w):
    return HEAT_TRANSFER * (1.0 + 0.5 * (u * u + v * v + w * w))


def iota(shape, dim):
    return lax.broadcasted_iota(I32, shape, dim)


def bits(mask):
    return jnp.where(mask, 1.0, 0.0).astype(BF16)


def dot(a, b):
    return lax.dot_general(a, b, (((1,), (0,)), ((), ())), preferred_element_type=F32)


def dot_t(a, b):
    return lax.dot_general(a, b, (((1,), (1,)), ((), ())), preferred_element_type=F32)


def kernel(
    state,
    prec,
    imap,
    fcell,
    fown,
    wall,
    out_state,
    out_flux,
    q0,
    q1,
    wv,
    pv,
    imv,
    fcv,
    fov,
    psend,
    win,
    wsend,
    wrecv,
    hy_send,
    hy_recv,
    hz_send,
    hz_recv,
    fsend,
    frecv,
    oh_cell,
    oh_slot,
    oh_in,
    oh_srow,
    vm,
    fm,
    lhs_0,
    lhs_1,
    wl,
    zf,
    qf,
    rf,
    lf,
    hf,
    sf,
    zi,
    hi_in,
    ri,
    rcell,
    rslot,
    count,
    s_sum,
    f_sum,
    later,
    a_face,
    b_face,
    t_face,
    i_face,
    f_face,
    found_0,
    found_1,
    load_sem,
    p_send_sem,
    p_recv_sem,
    w_send_sem,
    w_recv_sem,
    h_send_sem,
    h_recv_sem,
    f_send_sem,
    f_recv_sem,
):
    fl, inf, so = lax.axis_index("fluid"), lax.axis_index("inflow"), lax.axis_index("solid")

    loads = [
        pltpu.make_async_copy(prec, pv, load_sem.at[0]),
        pltpu.make_async_copy(wall, wv, load_sem.at[1]),
        pltpu.make_async_copy(fown, fov, load_sem.at[3]),
        pltpu.make_async_copy(fcell, fcv, load_sem.at[4]),
        pltpu.make_async_copy(imap, imv, load_sem.at[5]),
        pltpu.make_async_copy(state, q0.at[:, pl.ds(1, XL), pl.ds(TOP, CY)], load_sem.at[2]),
    ]
    for load in loads:
        load.start()

    barrier = pltpu.get_barrier_semaphore()

    def greet(ids):
        pl.semaphore_signal(barrier, inc=1, device_id=ids, device_id_type=MESH)

    for d in range(1, N_INFLOW):
        greet({"inflow": (inf + d) & (N_INFLOW - 1)})
    for d in (1, N_FLUID - 1):
        greet({"fluid": (fl + d) & (N_FLUID - 1)})
    for d in range(1, N_SOLID):
        greet({"solid": (so + d) & (N_SOLID - 1)})

    lane = iota((CY, CZ), 1)

    loads[0].wait()
    for s in range(2):
        for k in range(16):
            psend[s, pl.ds(k, 4, stride=16), :] = pv[s, :, k * 128 : (k + 1) * 128].astype(F32)
    for s in range(2):
        win[s, inf] = psend[s].astype(BF16)
    loads[1].wait()
    for t in range(64):
        wsend[pl.ds(t // 16 * 32 + t % 16, 2, stride=16), :] = wv[0:2, t * 128 : (t + 1) * 128]

    wall_copies = []
    for d in range(1, N_SOLID):
        to = (so + d) & (N_SOLID - 1)
        wall_copies.append(
            pltpu.make_async_remote_copy(
                src_ref=wsend.at[pl.ds(pl.multiple_of(to * 32, 32), 32)],
                dst_ref=wrecv.at[pl.ds(pl.multiple_of(so * 32, 32), 32)],
                send_sem=w_send_sem.at[d - 1],
                recv_sem=w_recv_sem.at[d - 1],
                device_id={"solid": to},
                device_id_type=MESH,
            )
        )

    def halo_copies(step):
        copies = []
        for side in range(2):
            far = N_FLUID - 1 if side == 0 else 1
            copies.append(
                pltpu.make_async_remote_copy(
                    src_ref=hy_send.at[step, side],
                    dst_ref=hy_recv.at[step, 1 - side],
                    send_sem=h_send_sem.at[step, 0, side],
                    recv_sem=h_recv_sem.at[step, 0, side],
                    device_id={"fluid": (fl + far) & (N_FLUID - 1)},
                    device_id_type=MESH,
                )
            )
        for side in range(2):
            far = N_INFLOW - 1 if side == 0 else 1
            copies.append(
                pltpu.make_async_remote_copy(
                    src_ref=hz_send.at[step],
                    dst_ref=hz_recv.at[step, 1 - side],
                    send_sem=h_send_sem.at[step, 1, side],
                    recv_sem=h_recv_sem.at[step, 1, side],
                    device_id={"inflow": (inf + far) & (N_INFLOW - 1)},
                    device_id_type=MESH,
                )
            )
        return copies

    precursor_copies = [
        pltpu.make_async_remote_copy(
            src_ref=win.at[:, inf],
            dst_ref=win.at[:, inf],
            send_sem=p_send_sem.at[d - 1],
            recv_sem=p_recv_sem.at[d - 1],
            device_id={"inflow": (inf + d) & (N_INFLOW - 1)},
            device_id_type=MESH,
        )
        for d in range(1, N_INFLOW)
    ]

    def precursor_arrivals():
        for d in range(1, N_INFLOW):
            came = (inf + N_INFLOW - d) & (N_INFLOW - 1)
            pltpu.make_async_remote_copy(
                src_ref=win.at[:, came],
                dst_ref=win.at[:, came],
                send_sem=p_send_sem.at[d - 1],
                recv_sem=p_recv_sem.at[d - 1],
                device_id={"inflow": came},
                device_id_type=MESH,
            ).wait_recv()

    def wall_arrivals():
        for d in range(1, N_SOLID):
            came = (so + N_SOLID - d) & (N_SOLID - 1)
            pltpu.make_async_remote_copy(
                src_ref=wsend.at[pl.ds(pl.multiple_of(came * 32, 32), 32)],
                dst_ref=wrecv.at[pl.ds(pl.multiple_of(came * 32, 32), 32)],
                send_sem=w_send_sem.at[d - 1],
                recv_sem=w_recv_sem.at[d - 1],
                device_id={"solid": came},
                device_id_type=MESH,
            ).wait_recv()

    def flux_arrivals():
        for d in range(1, N_SOLID):
            came = (so + N_SOLID - d) & (N_SOLID - 1)
            pltpu.make_async_remote_copy(
                src_ref=fsend.at[:, pl.ds(pl.multiple_of(came * 16, 16), 16)],
                dst_ref=frecv.at[:, pl.ds(pl.multiple_of(came * 16, 16), 16)],
                send_sem=f_send_sem.at[d - 1],
                recv_sem=f_recv_sem.at[d - 1],
                device_id={"solid": came},
                device_id_type=MESH,
            ).wait_recv()

    pl.semaphore_wait(barrier, (N_INFLOW - 1) + 2 + (N_SOLID - 1))
    for copy in wall_copies + precursor_copies:
        copy.start()

    def pair_of(c, x):
        return (c % 2) * XL + x

    def keep_edges(step, x, values, packed):
        packed = list(packed)
        for c in range(NV):
            k = c * XL + x
            hy_send[step, 0, pl.ds(k, 1), :] = values[c][0:1]
            hy_send[step, 1, pl.ds(k, 1), :] = values[c][CY - 1 : CY]
            j = pair_of(c, x)
            moved = pltpu.roll(values[c], 2 * j + 1, 1)
            packed[c // 2] = jnp.where(lax.shift_right_logical(lane, 1) == j, moved, packed[c // 2])
        return tuple(packed)

    zero_plane = jnp.zeros((CY, CZ), F32)
    lhs = (lhs_0, lhs_1)

    def keep_sample_plane(step, x, u, v, w, temp):
        (a_high, a_low), (b_high, b_low) = split(transfer_of(u, v, w)), split(temp)
        parts = (a_high, b_high, a_low, b_low)
        quarter = lax.shift_right_logical(x, 3)
        at = pl.multiple_of((x & 7) * CY, CY)
        for i, part in enumerate(parts):
            lhs[step][quarter, pl.ds(i * 128 + at, CY), :] = part

    for load in loads[2:5]:
        load.wait()
    cell = fcv[...]
    qf[...] = lax.shift_right_logical(cell, 14).astype(F32)
    zf[...] = (cell & 127).astype(F32)
    r = lax.shift_right_logical(cell, 7) & 127
    rcell[...] = r
    rf[...] = r.astype(F32)
    owner = fov[...]
    marks = jnp.concatenate([jnp.where(owner == o, 1.0, 0.0) for o in range(N_SOLID)], axis=0)
    upper = jnp.where(iota((128, 128), 0) < iota((128, 128), 1), 1.0, 0.0)
    earlier = dot(
        marks.astype(BF16), jnp.concatenate([upper, jnp.ones((128, 128), F32)], axis=1).astype(BF16)
    )
    r_out, r_in = iota((128, 128), 0), iota((128, 128), 1)
    same = lax.shift_right_logical(r_out, 5) == lax.shift_right_logical(r_in, 5)
    below = bits(jnp.logical_and(same, r_in < r_out))
    ranks = (earlier[:, :128] + dot(below, earlier[:, 128:].astype(BF16))) * marks
    rank = ranks[0:32] + ranks[32:64] + ranks[64:96] + ranks[96:128]
    slot = owner * CAP + rank.astype(I32)
    hi = lax.shift_right_logical(slot, 7)
    hf[...] = lax.shift_right_logical(hi, 5).astype(F32)
    lf[...] = (slot & 127).astype(F32)
    rslot[...] = hi & 31
    sf[...] = (hi & 31).astype(F32)
    relative = imv[...] - fl * (N_INFLOW * CAP)
    hi = lax.shift_right_logical(relative, 7)
    zi[...] = (relative & 127).astype(F32)
    hi_in[...] = lax.shift_right_logical(hi, 6).astype(F32)
    ri[...] = hi & 63

    steps_128 = iota((128, 128), 0).astype(F32).astype(BF16)
    one, zero = jnp.ones((), BF16), jnp.zeros((), BF16)

    def wide(row_values, blocks):
        tile = jnp.broadcast_to(row_values, (16, 128)).astype(BF16)
        return jnp.concatenate([tile] * blocks, axis=0) if blocks > 1 else tile

    def hot(row_values, blocks):
        return jnp.where(steps_128[: blocks * 16] == wide(row_values, blocks), one, zero)

    def marked(row_values, value, blocks):
        return wide(jnp.where(row_values == value, 1.0, 0.0), blocks)

    def lanes_of(j):
        return pl.ds(pl.multiple_of(j * 128, 128), 128)

    def one_hots_of_faces(j):
        at, cols = pl.ds(j, 1), lanes_of(j)
        base, quarter = hot(zf[at, :], 8), qf[at, :]
        for part in range(4):
            oh_cell[part * 128 : (part + 1) * 128, cols] = base * marked(quarter, float(part), 8)
        vm[0:128, cols] = hot(rf[at, :], 8)
        base, half = hot(lf[at, :], 8), hf[at, :]
        for part in range(2):
            oh_slot[part * 128 : (part + 1) * 128, cols] = base * marked(half, float(part), 8)
        oh_srow[:, cols] = hot(sf[at, :], 2)

    def one_hots_of_inlet(j):
        at, cols = pl.ds(j, 1), lanes_of(j)
        base, half = hot(zi[at, :], 8), hi_in[at, :]
        for part in range(2):
            oh_in[part * 128 : (part + 1) * 128, cols] = base * marked(half, float(part), 8)

    loads[5].wait()

    def prepare(n, packed):
        for i in range(4):
            x = n * 4 + i
            values = [q0[c, x + 1, TOP : TOP + CY, :] for c in range(NV)]
            keep_sample_plane(0, x, *values)
            packed = keep_edges(0, x, values, packed)
            one_hots_of_faces(n * 4 + i)
        for i in range(2):
            one_hots_of_inlet(n * 2 + i)
        return packed

    packed = lax.fori_loop(0, XL // 4, prepare, (zero_plane, zero_plane), unroll=4)
    hz_send[0, 0] = packed[0]
    hz_send[0, 1] = packed[1]
    halos_0 = halo_copies(0)
    for copy in halos_0:
        copy.start()
    for c in range(NV):
        q0[c, XL + 1, TOP : TOP + CY, :] = q0[c, XL, TOP : TOP + CY, :]

    def sample_product(step, n, found):
        cols = oh_cell[:, pl.ds(pl.multiple_of(n * CHUNK, CHUNK), CHUNK)]
        fields = jnp.concatenate([lhs[step][i] for i in range(4)], axis=1)
        both = dot(fields, cols)
        found[...] = both[0:256] + both[256:512]

    def sample_pick(n, found):
        for j in range(CHUNK // 128):
            at = n * (CHUNK // 128) + j
            cols = slice(j * 128, (j + 1) * 128)
            mask = iota((128, 128), 0) == rcell[pl.ds(at, 1), :]
            for ref, base in ((a_face, 0), (b_face, 128)):
                both = found[base : base + 128, cols]
                ref[pl.ds(at, 1), :] = jnp.sum(jnp.where(mask, both, 0.0), axis=0, keepdims=True)

    def sample_faces(step, beside, carry):
        sample_product(step, 0, found_0)

        def two(m, carry):
            sample_product(step, 2 * m + 1, found_1)
            carry = beside(2 * m, carry)
            sample_pick(2 * m, found_0)
            sample_product(step, (2 * m + 2) & (CHUNKS - 1), found_0)
            carry = beside(2 * m + 1, carry)
            sample_pick(2 * m + 1, found_1)
            return carry

        return lax.fori_loop(0, CHUNKS // 2, two, carry, unroll=CHUNKS // 2 if step == 0 else 2)

    own = pl.multiple_of(so * 32, 32)
    wrecv[pl.ds(own, 32)] = wsend[pl.ds(own, 32)]
    wall_arrivals()
    for o in range(N_SOLID):
        for layer in range(2):
            for i, part in enumerate(split(wrecv[o * 32 + layer * 16 : o * 32 + layer * 16 + 16, :])):
                at = (layer * 2 + i) * 32 + (o & 1) * 16
                wl[at : at + 16, (o >> 1) * 128 : (o >> 1) * 128 + 128] = part

    for n in range(FACES // 512):
        found = dot(wl[...], oh_slot[:, n * 512 : (n + 1) * 512])
        for j in range(4):
            at = n * 4 + j
            mask = iota((32, 128), 0) == rslot[at : at + 1, :]
            part = found[:, j * 128 : (j + 1) * 128]
            for ref, base in ((t_face, 0), (i_face, 64)):
                both = part[base : base + 32] + part[base + 32 : base + 64]
                ref[at : at + 1, :] = jnp.sum(jnp.where(mask, both, 0.0), axis=0, keepdims=True)
    t0 = t_face[...]
    t1 = i_face[...]
    between = 0.5 * (jnp.exp(CONDUCT_SLOPE * t0) + jnp.exp(CONDUCT_SLOPE * t1)) * (t1 - t0)
    i_face[...] = between

    def halves(x):
        high, low = split(x)
        return high.astype(F32), low.astype(F32)

    fields = halves(t0) + halves(between)
    for j in range(ROWS):
        cols = slice(j * 128, (j + 1) * 128)
        marks = vm[0:128, cols]
        for i, field in enumerate(fields):
            vm[(i + 1) * 128 : (i + 2) * 128, cols] = marks * wide(field[j : j + 1, :], 8)
    sums = dot_t(vm[...], oh_cell[...])
    for part in range(4):
        cols, rows = slice(part * 128, (part + 1) * 128), slice(part * 128, (part + 1) * 128)
        count[rows, :] = sums[0:128, cols]
        s_sum[rows, :] = sums[128:256, cols] + sums[256:384, cols]
        f_sum[rows, :] = sums[384:512, cols] + sums[512:640, cols]

    precursor_arrivals()
    window = jnp.concatenate(
        [
            jnp.concatenate(
                [win[step, 0:4].reshape(256, 128), win[step, 4:8].reshape(256, 128)], axis=1
            )
            for step in range(2)
        ],
        axis=0,
    )
    for g in range(CY // 4):
        found = dot(window, oh_in[:, g * 512 : (g + 1) * 512])
        for j in range(4):
            y = g * 4 + j
            mask = iota((64, 128), 0) == ri[y : y + 1, :]
            for step, dst in ((0, q0), (1, q1)):
                part = found[step * 256 : (step + 1) * 256, j * 128 : (j + 1) * 128]
                for c in range(NV):
                    total = None
                    for src in range(4):
                        term = jnp.where(
                            mask[src * 16 : src * 16 + 16],
                            part[src * 64 + c * 16 : src * 64 + c * 16 + 16],
                            0.0,
                        )
                        total = term if total is None else total + term
                    dst[c, 0, TOP + y : TOP + y + 1, :] = jnp.sum(total, axis=0, keepdims=True)

    def receive_halos(step, copies, dst):
        for copy in copies:
            copy.wait_recv()

        def rows_of(x, _):
            for c in range(NV):
                k = c * XL + x
                dst[c, x + 1, TOP - 1 : TOP, :] = jnp.where(
                    fl > 0, hy_recv[step, 0, pl.ds(k, 1), :], 0.0
                )
                dst[c, x + 1, TOP + CY : TOP + CY + 1, :] = jnp.where(
                    fl < N_FLUID - 1, hy_recv[step, 1, pl.ds(k, 1), :], 0.0
                )
            return 0

        lax.fori_loop(0, XL, rows_of, 0, unroll=32)
        merged = []
        for part in range(2):
            low = jnp.where(inf > 0, pltpu.roll(hz_recv[step, 0, part], 1, 1), 0.0)
            high = jnp.where(inf < N_INFLOW - 1, pltpu.roll(hz_recv[step, 1, part], 127, 1), 0.0)
            merged.append(jnp.where((lane & 1) == 1, low, high))
        return merged

    first_lane, last_lane = lane == 0, lane == CZ - 1

    def advanced(src, merged, x):
        centre = [src[c, x + 1, TOP : TOP + CY, :] for c in range(NV)]
        half = 0.5 * TIME_STEP
        slopes = [half * speed for speed in centre[:3]]
        ahead = [VISCOSITY * TIME_STEP - slope for slope in slopes]
        behind = [VISCOSITY * TIME_STEP + slope for slope in slopes]
        fresh = []
        for c in range(NV):
            q = centre[c]
            j = pair_of(c, x)
            edge = pltpu.roll(merged[c // 2], 127 - 2 * j, 1)
            zm = jnp.where(first_lane, edge, pltpu.roll(q, 1, 1))
            zp = jnp.where(last_lane, edge, pltpu.roll(q, CZ - 1, 1))
            xm = src[c, x, TOP : TOP + CY, :]
            xp = src[c, x + 2, TOP : TOP + CY, :]
            ym = src[c, x + 1, TOP - 1 : TOP + CY - 1, :]
            yp = src[c, x + 1, TOP + 1 : TOP + CY + 1, :]
            along_x = ahead[0] * xp + behind[0] * xm
            along_y = ahead[1] * yp + behind[1] * ym
            along_z = ahead[2] * zp + behind[2] * zm
            fresh.append(
                (1.0 - 6.0 * VISCOSITY * TIME_STEP) * q + ((along_x + along_y) + along_z)
            )
        return centre, fresh

    merged_0 = receive_halos(0, halos_0, q0)

    def first(n, packed):
        for i in range(PLANES):
            x = n * PLANES + i
            rows = pl.ds(pl.multiple_of(x * CY, CY), CY)
            centre, fresh = advanced(q0, merged_0, x)
            u, v, w, temp = centre
            colder = s_sum[rows, :]
            total = transfer_of(u, v, w) * (count[rows, :] * temp - colder)
            later[rows, :] = colder + SOLID_STEP * (f_sum[rows, :] + total)
            fresh[3] = fresh[3] - WALL_WEIGHT * total
            for c in range(NV):
                q1[c, x + 1, TOP : TOP + CY, :] = fresh[c]
            keep_sample_plane(1, x, *fresh)
            packed = keep_edges(1, x, fresh, packed)
        return packed

    packed = sample_faces(0, first, (zero_plane, zero_plane))
    hz_send[1, 0] = packed[0]
    hz_send[1, 1] = packed[1]
    halos_1 = halo_copies(1)
    for copy in halos_1:
        copy.start()
    for c in range(NV):
        q1[c, XL + 1, TOP : TOP + CY, :] = q1[c, XL, TOP : TOP + CY, :]

    flux_0 = a_face[...] * (b_face[...] - t_face[...])
    t_face[...] = t_face[...] + SOLID_STEP * (i_face[...] + flux_0)
    f_face[...] = flux_0
    sample_faces(1, lambda n, carry: carry, 0)
    parts = halves(f_face[...]) + halves(a_face[...] * (b_face[...] - t_face[...]))
    for j in range(ROWS):
        cols = slice(j * 128, (j + 1) * 128)
        marks = oh_srow[:, cols]
        for i, part in enumerate(parts):
            fm[i * 32 : (i + 1) * 32, cols] = marks * wide(part[j : j + 1, :], 2)
    found = jnp.transpose(dot_t(oh_slot[...], fm[...]))
    for step in range(2):
        both = found[step * 64 : step * 64 + 32] + found[step * 64 + 32 : step * 64 + 64]
        for o in range(N_SOLID):
            fsend[step, o * 16 : (o + 1) * 16] = both[
                (o & 1) * 16 : (o & 1) * 16 + 16, (o >> 1) * 128 : (o >> 1) * 128 + 128
            ]
    flux_copies = []
    for d in range(1, N_SOLID):
        to = (so + d) & (N_SOLID - 1)
        flux_copies.append(
            pltpu.make_async_remote_copy(
                src_ref=fsend.at[:, pl.ds(pl.multiple_of(to * 16, 16), 16)],
                dst_ref=frecv.at[:, pl.ds(pl.multiple_of(so * 16, 16), 16)],
                send_sem=f_send_sem.at[d - 1],
                recv_sem=f_recv_sem.at[d - 1],
                device_id={"solid": to},
                device_id_type=MESH,
            )
        )
    for copy in flux_copies:
        copy.start()
    own = pl.multiple_of(so * 16, 16)
    for step in range(2):
        frecv[step, pl.ds(own, 16)] = fsend[step, pl.ds(own, 16)]

    merged_1 = receive_halos(1, halos_1, q1)

    def second(x, _):
        rows = pl.ds(pl.multiple_of(x * CY, CY), CY)
        centre, fresh = advanced(q1, merged_1, x)
        u, v, w, temp = centre
        total = transfer_of(u, v, w) * (count[rows, :] * temp - later[rows, :])
        fresh[3] = fresh[3] - WALL_WEIGHT * total
        for c in range(NV):
            out_state[c, x] = fresh[c]
        return 0

    lax.fori_loop(0, XL, second, 0, unroll=16)
    flux_arrivals()
    out_flux[...] = frecv[...]
    for copy in wall_copies + precursor_copies + halos_0 + halos_1 + flux_copies:
        copy.wait_send()


def finish(fluid, fv, wall, out_state, out_wall, wv, out_sem):
    outs = [pltpu.make_async_copy(fluid.at[c], out_state.at[c], out_sem.at[c]) for c in range(NV)]
    for copy in outs:
        copy.start()
    layer = iota((LAYERS, 128), 0)

    def conduct(temps, flux_row):
        conductivity = jnp.exp(CONDUCT_SLOPE * temps)
        above = pltpu.roll(temps, LAYERS - 1, 0)
        c_above = pltpu.roll(conductivity, LAYERS - 1, 0)
        flow = jnp.where(
            layer == LAYERS - 1,
            conductivity * (0.0 - temps),
            0.5 * (conductivity + c_above) * (above - temps),
        )
        from_below = jnp.where(layer == 0, flux_row, -pltpu.roll(flow, 1, 0))
        return temps + SOLID_STEP * (flow + from_below)

    for part in range(4):
        cols = [slice((part * 16 + i) * 128, (part * 16 + i + 1) * 128) for i in range(16)]
        temps = [wall[:, col] for col in cols]
        for step in range(2):
            rows = [fv[step, part * 16 + i : part * 16 + i + 1, :] for i in range(16)]
            temps = [conduct(temp, flux_row) for temp, flux_row in zip(temps, rows)]
        for col, temp in zip(cols, temps):
            wv[:, col] = temp
        span = slice(part * 2048, (part + 1) * 2048)
        outs.append(pltpu.make_async_copy(wv.at[:, span], out_wall.at[:, span], out_sem.at[NV + part]))
        outs[-1].start()
    for copy in outs:
        copy.wait()


def local(state, precursor, inlet_map, face_cell, face_owner, wall_temp):
    any_space = pl.BlockSpec(memory_space=pl.ANY)
    vmem = pltpu.VMEM
    dma = pltpu.SemaphoreType.DMA
    fluid, flux = pl.pallas_call(
        kernel,
        out_shape=(vmem((NV, XL, CY, CZ), F32), vmem((2, 64, 128), F32)),
        in_specs=[any_space] * 6,
        out_specs=(pl.BlockSpec(memory_space=vmem),) * 2,
        scratch_shapes=[
            vmem((NV, XL + 2, PITCH, CZ), F32),
            vmem((NV, XL + 2, PITCH, CZ), F32),
            vmem((LAYERS, COLUMNS), F32),
            vmem((2, NV, CAP), BF16),
            vmem((CY, CZ), I32),
            vmem((ROWS, 128), I32),
            vmem((ROWS, 128), I32),
            vmem((2, 64, 128), F32),
            vmem((2, N_INFLOW, 64, 128), BF16),
            vmem((128, 128), F32),
            vmem((128, 128), F32),
            vmem((2, 2, 128, 128), F32),
            vmem((2, 2, 128, 128), F32),
            vmem((2, 2, CY, 128), F32),
            vmem((2, 2, 2, CY, 128), F32),
            vmem((2, 64, 128), F32),
            vmem((2, 64, 128), F32),
            vmem((512, FACES), BF16),
            vmem((256, FACES), BF16),
            vmem((256, CY * CZ), BF16),
            vmem((32, FACES), BF16),
            vmem((640, FACES), BF16),
            vmem((128, FACES), BF16),
            vmem((4, 512, 128), BF16),
            vmem((4, 512, 128), BF16),
            vmem((128, 256), BF16),
            vmem((ROWS, 128), F32),
            vmem((ROWS, 128), F32),
            vmem((ROWS, 128), F32),
            vmem((ROWS, 128), F32),
            vmem((ROWS, 128), F32),
            vmem((ROWS, 128), F32),
            vmem((CY, 128), F32),
            vmem((CY, 128), F32),
            vmem((CY, 128), I32),
            vmem((ROWS, 128), I32),
            vmem((ROWS, 128), I32),
            vmem((512, 128), F32),
            vmem((512, 128), F32),
            vmem((512, 128), F32),
            vmem((512, 128), F32),
            vmem((ROWS, 128), F32),
            vmem((ROWS, 128), F32),
            vmem((ROWS, 128), F32),
            vmem((ROWS, 128), F32),
            vmem((ROWS, 128), F32),
            vmem((256, CHUNK), F32),
            vmem((256, CHUNK), F32),
            dma((6,)),
            dma((N_INFLOW - 1,)),
            dma((N_INFLOW - 1,)),
            dma((N_SOLID - 1,)),
            dma((N_SOLID - 1,)),
            dma((2, 2, 2)),
            dma((2, 2, 2)),
            dma((N_SOLID - 1,)),
            dma((N_SOLID - 1,)),
        ],
        compiler_params=pltpu.CompilerParams(
            collective_id=0, has_side_effects=True, vmem_limit_bytes=60 * 1024 * 1024
        ),
        name="manifold_step",
    )(
        state[0],
        precursor[0],
        inlet_map[0],
        face_cell.reshape(ROWS, 128),
        face_owner.reshape(ROWS, 128),
        wall_temp[0, 0, 0],
    )
    new_state, new_wall = pl.pallas_call(
        finish,
        out_shape=(
            jax.ShapeDtypeStruct((NV, XL, CY, CZ), F32),
            jax.ShapeDtypeStruct((LAYERS, COLUMNS), F32),
        ),
        in_specs=[any_space] + [pl.BlockSpec(memory_space=vmem)] * 2,
        out_specs=(any_space, any_space),
        scratch_shapes=[
            vmem((LAYERS, COLUMNS), F32),
            dma((2 * NV,)),
        ],
        compiler_params=pltpu.CompilerParams(vmem_limit_bytes=8 * 1024 * 1024),
        name="finish",
    )(fluid, flux, wall_temp[0, 0, 0])
    return new_state[None], new_wall[None, None, None]


def solution(mesh):
    return jax.shard_map(
        local,
        mesh=mesh,
        in_specs=(
            P("solid", None, None, "fluid", "inflow"),
            P("solid", None, None, ("fluid", "inflow")),
            P("solid", "fluid", "inflow"),
            P("solid", "fluid", "inflow", None),
            P("solid", "fluid", "inflow", None, None),
            P("solid", "fluid", "inflow", None, None),
        ),
        out_specs=(
            P("solid", None, None, "fluid", "inflow"),
            P("solid", "fluid", "inflow", None, None),
        ),
        check_vma=False,
    )
```

```python
import functools

import jax
import jax.numpy as jnp
from jax import lax
from jax.experimental import pallas as pl
from jax.experimental.pallas import tpu as pltpu
from jax.sharding import PartitionSpec as P

F32, BF16, I32 = jnp.float32, jnp.bfloat16, jnp.int32
MESH = pl.DeviceIdType.MESH

XL, CY, CZ, NV = 32, 16, 128, 4
CAP, LAYERS, FACES = 2048, 8, 4096
N_FLUID, N_INFLOW, N_SOLID = 8, 8, 4
COLUMNS = N_SOLID * CAP
ROWS = FACES // 128
TOP, PITCH = 8, 32
CHUNK = 512
CHUNKS = FACES // CHUNK
PLANES = XL // CHUNKS

TIME_STEP = 0.1
VISCOSITY = 0.5
HEAT_TRANSFER = 0.8
CONDUCT_SLOPE = 0.2
SOLID_STEP = 0.15
WALL_WEIGHT = 0.5


def split(x):
    high = x.astype(BF16)
    return high, (x - high.astype(F32)).astype(BF16)


def transfer_of(u, v, w):
    return HEAT_TRANSFER * (1.0 + 0.5 * (u * u + v * v + w * w))


def iota(shape, dim):
    return lax.broadcasted_iota(I32, shape, dim)


def bits(mask):
    return jnp.where(mask, 1.0, 0.0).astype(BF16)


def dot(a, b):
    return lax.dot_general(a, b, (((1,), (0,)), ((), ())), preferred_element_type=F32)


def dot_t(a, b):
    return lax.dot_general(a, b, (((1,), (1,)), ((), ())), preferred_element_type=F32)


def kernel(
    state,
    prec,
    imap,
    fcell,
    fown,
    wall,
    out_state,
    out_flux,
    q0,
    q1,
    wv,
    pv,
    imv,
    fcv,
    fov,
    psend,
    win,
    wsend,
    wrecv,
    hy_send,
    hy_recv,
    hz_send,
    hz_recv,
    fsend,
    frecv,
    oh_cell,
    oh_slot,
    oh_in,
    oh_srow,
    vm,
    fm,
    lhs_0,
    lhs_1,
    wl,
    zf,
    qf,
    rf,
    lf,
    hf,
    sf,
    zi,
    hi_in,
    ri,
    rcell,
    rslot,
    count,
    s_sum,
    f_sum,
    later,
    a_face,
    b_face,
    t_face,
    i_face,
    f_face,
    found_0,
    found_1,
    load_sem,
    p_send_sem,
    p_recv_sem,
    w_send_sem,
    w_recv_sem,
    h_send_sem,
    h_recv_sem,
    f_send_sem,
    f_recv_sem,
):
    fl, inf, so = lax.axis_index("fluid"), lax.axis_index("inflow"), lax.axis_index("solid")

    loads = [
        pltpu.make_async_copy(prec, pv, load_sem.at[0]),
        pltpu.make_async_copy(wall, wv, load_sem.at[1]),
        pltpu.make_async_copy(fown, fov, load_sem.at[3]),
        pltpu.make_async_copy(fcell, fcv, load_sem.at[4]),
        pltpu.make_async_copy(imap, imv, load_sem.at[5]),
        pltpu.make_async_copy(state, q0.at[:, pl.ds(1, XL), pl.ds(TOP, CY)], load_sem.at[2]),
    ]

    barrier = pltpu.get_barrier_semaphore()

    def greet(ids):
        pl.semaphore_signal(barrier, inc=1, device_id=ids, device_id_type=MESH)

    for d in range(1, N_INFLOW):
        greet({"inflow": (inf + d) & (N_INFLOW - 1)})
    for d in (1, N_FLUID - 1):
        greet({"fluid": (fl + d) & (N_FLUID - 1)})
    for d in range(1, N_SOLID):
        greet({"solid": (so + d) & (N_SOLID - 1)})

    for load in loads:
        load.start()

    lane = iota((CY, CZ), 1)

    loads[0].wait()
    for s in range(2):
        for k in range(16):
            psend[s, pl.ds(k, 4, stride=16), :] = pv[s, :, k * 128 : (k + 1) * 128].astype(F32)
    for s in range(2):
        win[s, inf] = psend[s].astype(BF16)
    loads[1].wait()
    for t in range(64):
        wsend[pl.ds(t // 16 * 32 + t % 16, 2, stride=16), :] = wv[0:2, t * 128 : (t + 1) * 128]

    wall_copies = []
    for d in range(1, N_SOLID):
        to = (so + d) & (N_SOLID - 1)
        wall_copies.append(
            pltpu.make_async_remote_copy(
                src_ref=wsend.at[pl.ds(pl.multiple_of(to * 32, 32), 32)],
                dst_ref=wrecv.at[pl.ds(pl.multiple_of(so * 32, 32), 32)],
                send_sem=w_send_sem.at[d - 1],
                recv_sem=w_recv_sem.at[d - 1],
                device_id={"solid": to},
                device_id_type=MESH,
            )
        )

    def halo_copies(step):
        copies = []
        for side in range(2):
            far = N_FLUID - 1 if side == 0 else 1
            copies.append(
                pltpu.make_async_remote_copy(
                    src_ref=hy_send.at[step, side],
                    dst_ref=hy_recv.at[step, 1 - side],
                    send_sem=h_send_sem.at[step, 0, side],
                    recv_sem=h_recv_sem.at[step, 0, side],
                    device_id={"fluid": (fl + far) & (N_FLUID - 1)},
                    device_id_type=MESH,
                )
            )
        for side in range(2):
            far = N_INFLOW - 1 if side == 0 else 1
            copies.append(
                pltpu.make_async_remote_copy(
                    src_ref=hz_send.at[step],
                    dst_ref=hz_recv.at[step, 1 - side],
                    send_sem=h_send_sem.at[step, 1, side],
                    recv_sem=h_recv_sem.at[step, 1, side],
                    device_id={"inflow": (inf + far) & (N_INFLOW - 1)},
                    device_id_type=MESH,
                )
            )
        return copies

    precursor_copies = [
        pltpu.make_async_remote_copy(
            src_ref=win.at[:, inf],
            dst_ref=win.at[:, inf],
            send_sem=p_send_sem.at[d - 1],
            recv_sem=p_recv_sem.at[d - 1],
            device_id={"inflow": (inf + d) & (N_INFLOW - 1)},
            device_id_type=MESH,
        )
        for d in range(1, N_INFLOW)
    ]

    def precursor_arrivals():
        for d in range(1, N_INFLOW):
            came = (inf + N_INFLOW - d) & (N_INFLOW - 1)
            pltpu.make_async_remote_copy(
                src_ref=win.at[:, came],
                dst_ref=win.at[:, came],
                send_sem=p_send_sem.at[d - 1],
                recv_sem=p_recv_sem.at[d - 1],
                device_id={"inflow": came},
                device_id_type=MESH,
            ).wait_recv()

    def wall_arrivals():
        for d in range(1, N_SOLID):
            came = (so + N_SOLID - d) & (N_SOLID - 1)
            pltpu.make_async_remote_copy(
                src_ref=wsend.at[pl.ds(pl.multiple_of(came * 32, 32), 32)],
                dst_ref=wrecv.at[pl.ds(pl.multiple_of(came * 32, 32), 32)],
                send_sem=w_send_sem.at[d - 1],
                recv_sem=w_recv_sem.at[d - 1],
                device_id={"solid": came},
                device_id_type=MESH,
            ).wait_recv()

    def flux_arrivals():
        for d in range(1, N_SOLID):
            came = (so + N_SOLID - d) & (N_SOLID - 1)
            pltpu.make_async_remote_copy(
                src_ref=fsend.at[:, pl.ds(pl.multiple_of(came * 16, 16), 16)],
                dst_ref=frecv.at[:, pl.ds(pl.multiple_of(came * 16, 16), 16)],
                send_sem=f_send_sem.at[d - 1],
                recv_sem=f_recv_sem.at[d - 1],
                device_id={"solid": came},
                device_id_type=MESH,
            ).wait_recv()

    for load in loads[2:5]:
        load.wait()
    cell = fcv[...]
    qf[...] = lax.shift_right_logical(cell, 14).astype(F32)
    zf[...] = (cell & 127).astype(F32)
    r = lax.shift_right_logical(cell, 7) & 127
    rcell[...] = r
    rf[...] = r.astype(F32)
    owner = fov[...]
    marks = jnp.concatenate([jnp.where(owner == o, 1.0, 0.0) for o in range(N_SOLID)], axis=0)
    upper = jnp.where(iota((128, 128), 0) < iota((128, 128), 1), 1.0, 0.0)
    earlier = dot(
        marks.astype(BF16), jnp.concatenate([upper, jnp.ones((128, 128), F32)], axis=1).astype(BF16)
    )
    r_out, r_in = iota((128, 128), 0), iota((128, 128), 1)
    same = lax.shift_right_logical(r_out, 5) == lax.shift_right_logical(r_in, 5)
    below = bits(jnp.logical_and(same, r_in < r_out))
    ranks = (earlier[:, :128] + dot(below, earlier[:, 128:].astype(BF16))) * marks
    rank = ranks[0:32] + ranks[32:64] + ranks[64:96] + ranks[96:128]
    slot = owner * CAP + rank.astype(I32)
    hi = lax.shift_right_logical(slot, 7)
    hf[...] = lax.shift_right_logical(hi, 5).astype(F32)
    lf[...] = (slot & 127).astype(F32)
    rslot[...] = hi & 31
    sf[...] = (hi & 31).astype(F32)
    relative = imv[...] - fl * (N_INFLOW * CAP)
    hi = lax.shift_right_logical(relative, 7)
    zi[...] = (relative & 127).astype(F32)
    hi_in[...] = lax.shift_right_logical(hi, 6).astype(F32)
    ri[...] = hi & 63

    pl.semaphore_wait(barrier, (N_INFLOW - 1) + 2 + (N_SOLID - 1))
    for copy in wall_copies + precursor_copies:
        copy.start()

    def pair_of(c, x):
        return (c % 2) * XL + x

    def keep_edges(step, x, values, packed):
        packed = list(packed)
        for c in range(NV):
            k = c * XL + x
            hy_send[step, 0, pl.ds(k, 1), :] = values[c][0:1]
            hy_send[step, 1, pl.ds(k, 1), :] = values[c][CY - 1 : CY]
            j = pair_of(c, x)
            moved = pltpu.roll(values[c], 2 * j + 1, 1)
            packed[c // 2] = jnp.where(lax.shift_right_logical(lane, 1) == j, moved, packed[c // 2])
        return tuple(packed)

    zero_plane = jnp.zeros((CY, CZ), F32)
    lhs = (lhs_0, lhs_1)

    def keep_sample_plane(step, x, u, v, w, temp):
        (a_high, a_low), (b_high, b_low) = split(transfer_of(u, v, w)), split(temp)
        parts = (a_high, b_high, a_low, b_low)
        quarter = lax.shift_right_logical(x, 3)
        at = pl.multiple_of((x & 7) * CY, CY)
        for i, part in enumerate(parts):
            lhs[step][quarter, pl.ds(i * 128 + at, CY), :] = part

    steps_128 = iota((128, 128), 0).astype(F32).astype(BF16)
    one, zero = jnp.ones((), BF16), jnp.zeros((), BF16)

    def wide(row_values, blocks):
        tile = jnp.broadcast_to(row_values, (16, 128)).astype(BF16)
        return jnp.concatenate([tile] * blocks, axis=0) if blocks > 1 else tile

    def hot(row_values, blocks):
        return jnp.where(steps_128[: blocks * 16] == wide(row_values, blocks), one, zero)

    def marked(row_values, value, blocks):
        return wide(jnp.where(row_values == value, 1.0, 0.0), blocks)

    def lanes_of(j):
        return pl.ds(pl.multiple_of(j * 128, 128), 128)

    def one_hots_of_faces(j):
        at, cols = pl.ds(j, 1), lanes_of(j)
        base, quarter = hot(zf[at, :], 8), qf[at, :]
        for part in range(4):
            oh_cell[part * 128 : (part + 1) * 128, cols] = base * marked(quarter, float(part), 8)
        vm[0:128, cols] = hot(rf[at, :], 8)
        base, half = hot(lf[at, :], 8), hf[at, :]
        for part in range(2):
            oh_slot[part * 128 : (part + 1) * 128, cols] = base * marked(half, float(part), 8)
        oh_srow[:, cols] = hot(sf[at, :], 2)

    def one_hots_of_inlet(j):
        at, cols = pl.ds(j, 1), lanes_of(j)
        base, half = hot(zi[at, :], 8), hi_in[at, :]
        for part in range(2):
            oh_in[part * 128 : (part + 1) * 128, cols] = base * marked(half, float(part), 8)

    loads[5].wait()

    def prepare(n, packed):
        for i in range(4):
            x = n * 4 + i
            values = [q0[c, x + 1, TOP : TOP + CY, :] for c in range(NV)]
            keep_sample_plane(0, x, *values)
            packed = keep_edges(0, x, values, packed)
            one_hots_of_faces(n * 4 + i)
        for i in range(2):
            one_hots_of_inlet(n * 2 + i)
        return packed

    packed = lax.fori_loop(0, XL // 4, prepare, (zero_plane, zero_plane), unroll=4)
    hz_send[0, 0] = packed[0]
    hz_send[0, 1] = packed[1]
    halos_0 = halo_copies(0)
    for copy in halos_0:
        copy.start()
    for c in range(NV):
        q0[c, XL + 1, TOP : TOP + CY, :] = q0[c, XL, TOP : TOP + CY, :]

    def sample_product(step, n, found):
        cols = oh_cell[:, pl.ds(pl.multiple_of(n * CHUNK, CHUNK), CHUNK)]
        fields = jnp.concatenate([lhs[step][i] for i in range(4)], axis=1)
        both = dot(fields, cols)
        found[...] = both[0:256] + both[256:512]

    def sample_pick(n, found):
        for j in range(CHUNK // 128):
            at = n * (CHUNK // 128) + j
            cols = slice(j * 128, (j + 1) * 128)
            mask = iota((128, 128), 0) == rcell[pl.ds(at, 1), :]
            for ref, base in ((a_face, 0), (b_face, 128)):
                both = found[base : base + 128, cols]
                ref[pl.ds(at, 1), :] = jnp.sum(jnp.where(mask, both, 0.0), axis=0, keepdims=True)

    def sample_faces(step, beside, carry):
        sample_product(step, 0, found_0)

        def two(m, carry):
            sample_product(step, 2 * m + 1, found_1)
            carry = beside(2 * m, carry)
            sample_pick(2 * m, found_0)
            sample_product(step, (2 * m + 2) & (CHUNKS - 1), found_0)
            carry = beside(2 * m + 1, carry)
            sample_pick(2 * m + 1, found_1)
            return carry

        return lax.fori_loop(0, CHUNKS // 2, two, carry, unroll=CHUNKS // 2 if step == 0 else 2)

    own = pl.multiple_of(so * 32, 32)
    wrecv[pl.ds(own, 32)] = wsend[pl.ds(own, 32)]
    wall_arrivals()
    for o in range(N_SOLID):
        for layer in range(2):
            for i, part in enumerate(split(wrecv[o * 32 + layer * 16 : o * 32 + layer * 16 + 16, :])):
                at = (layer * 2 + i) * 32 + (o & 1) * 16
                wl[at : at + 16, (o >> 1) * 128 : (o >> 1) * 128 + 128] = part

    for n in range(FACES // 512):
        found = dot(wl[...], oh_slot[:, n * 512 : (n + 1) * 512])
        for j in range(4):
            at = n * 4 + j
            mask = iota((32, 128), 0) == rslot[at : at + 1, :]
            part = found[:, j * 128 : (j + 1) * 128]
            for ref, base in ((t_face, 0), (i_face, 64)):
                both = part[base : base + 32] + part[base + 32 : base + 64]
                ref[at : at + 1, :] = jnp.sum(jnp.where(mask, both, 0.0), axis=0, keepdims=True)
    t0 = t_face[...]
    t1 = i_face[...]
    between = 0.5 * (jnp.exp(CONDUCT_SLOPE * t0) + jnp.exp(CONDUCT_SLOPE * t1)) * (t1 - t0)
    i_face[...] = between

    def halves(x):
        high, low = split(x)
        return high.astype(F32), low.astype(F32)

    fields = halves(t0) + halves(between)
    for j in range(ROWS):
        cols = slice(j * 128, (j + 1) * 128)
        marks = vm[0:128, cols]
        for i, field in enumerate(fields):
            vm[(i + 1) * 128 : (i + 2) * 128, cols] = marks * wide(field[j : j + 1, :], 8)
    sums = dot_t(vm[...], oh_cell[...])
    for part in range(4):
        cols, rows = slice(part * 128, (part + 1) * 128), slice(part * 128, (part + 1) * 128)
        count[rows, :] = sums[0:128, cols]
        s_sum[rows, :] = sums[128:256, cols] + sums[256:384, cols]
        f_sum[rows, :] = sums[384:512, cols] + sums[512:640, cols]

    precursor_arrivals()
    window = jnp.concatenate(
        [
            jnp.concatenate(
                [win[step, 0:4].reshape(256, 128), win[step, 4:8].reshape(256, 128)], axis=1
            )
            for step in range(2)
        ],
        axis=0,
    )
    for g in range(CY // 4):
        found = dot(window, oh_in[:, g * 512 : (g + 1) * 512])
        for j in range(4):
            y = g * 4 + j
            mask = iota((64, 128), 0) == ri[y : y + 1, :]
            for step, dst in ((0, q0), (1, q1)):
                part = found[step * 256 : (step + 1) * 256, j * 128 : (j + 1) * 128]
                for c in range(NV):
                    total = None
                    for src in range(4):
                        term = jnp.where(
                            mask[src * 16 : src * 16 + 16],
                            part[src * 64 + c * 16 : src * 64 + c * 16 + 16],
                            0.0,
                        )
                        total = term if total is None else total + term
                    dst[c, 0, TOP + y : TOP + y + 1, :] = jnp.sum(total, axis=0, keepdims=True)

    def receive_halos(step, copies, dst):
        for copy in copies:
            copy.wait_recv()

        def rows_of(x, _):
            for c in range(NV):
                k = c * XL + x
                dst[c, x + 1, TOP - 1 : TOP, :] = jnp.where(
                    fl > 0, hy_recv[step, 0, pl.ds(k, 1), :], 0.0
                )
                dst[c, x + 1, TOP + CY : TOP + CY + 1, :] = jnp.where(
                    fl < N_FLUID - 1, hy_recv[step, 1, pl.ds(k, 1), :], 0.0
                )
            return 0

        lax.fori_loop(0, XL, rows_of, 0, unroll=32)
        merged = []
        for part in range(2):
            low = jnp.where(inf > 0, pltpu.roll(hz_recv[step, 0, part], 1, 1), 0.0)
            high = jnp.where(inf < N_INFLOW - 1, pltpu.roll(hz_recv[step, 1, part], 127, 1), 0.0)
            merged.append(jnp.where((lane & 1) == 1, low, high))
        return merged

    first_lane, last_lane = lane == 0, lane == CZ - 1

    def advanced(src, merged, x):
        centre = [src[c, x + 1, TOP : TOP + CY, :] for c in range(NV)]
        half = 0.5 * TIME_STEP
        slopes = [half * speed for speed in centre[:3]]
        ahead = [VISCOSITY * TIME_STEP - slope for slope in slopes]
        behind = [VISCOSITY * TIME_STEP + slope for slope in slopes]
        fresh = []
        for c in range(NV):
            q = centre[c]
            j = pair_of(c, x)
            edge = pltpu.roll(merged[c // 2], 127 - 2 * j, 1)
            zm = jnp.where(first_lane, edge, pltpu.roll(q, 1, 1))
            zp = jnp.where(last_lane, edge, pltpu.roll(q, CZ - 1, 1))
            xm = src[c, x, TOP : TOP + CY, :]
            xp = src[c, x + 2, TOP : TOP + CY, :]
            ym = src[c, x + 1, TOP - 1 : TOP + CY - 1, :]
            yp = src[c, x + 1, TOP + 1 : TOP + CY + 1, :]
            along_x = ahead[0] * xp + behind[0] * xm
            along_y = ahead[1] * yp + behind[1] * ym
            along_z = ahead[2] * zp + behind[2] * zm
            fresh.append(
                (1.0 - 6.0 * VISCOSITY * TIME_STEP) * q + ((along_x + along_y) + along_z)
            )
        return centre, fresh

    merged_0 = receive_halos(0, halos_0, q0)

    def first(n, packed):
        for i in range(PLANES):
            x = n * PLANES + i
            rows = pl.ds(pl.multiple_of(x * CY, CY), CY)
            centre, fresh = advanced(q0, merged_0, x)
            u, v, w, temp = centre
            colder = s_sum[rows, :]
            total = transfer_of(u, v, w) * (count[rows, :] * temp - colder)
            later[rows, :] = colder + SOLID_STEP * (f_sum[rows, :] + total)
            fresh[3] = fresh[3] - WALL_WEIGHT * total
            for c in range(NV):
                q1[c, x + 1, TOP : TOP + CY, :] = fresh[c]
            keep_sample_plane(1, x, *fresh)
            packed = keep_edges(1, x, fresh, packed)
        return packed

    packed = sample_faces(0, first, (zero_plane, zero_plane))
    hz_send[1, 0] = packed[0]
    hz_send[1, 1] = packed[1]
    halos_1 = halo_copies(1)
    for copy in halos_1:
        copy.start()
    for c in range(NV):
        q1[c, XL + 1, TOP : TOP + CY, :] = q1[c, XL, TOP : TOP + CY, :]

    flux_0 = a_face[...] * (b_face[...] - t_face[...])
    t_face[...] = t_face[...] + SOLID_STEP * (i_face[...] + flux_0)
    f_face[...] = flux_0
    sample_faces(1, lambda n, carry: carry, 0)
    parts = halves(f_face[...]) + halves(a_face[...] * (b_face[...] - t_face[...]))
    for j in range(ROWS):
        cols = slice(j * 128, (j + 1) * 128)
        marks = oh_srow[:, cols]
        for i, part in enumerate(parts):
            fm[i * 32 : (i + 1) * 32, cols] = marks * wide(part[j : j + 1, :], 2)
    found = jnp.transpose(dot_t(oh_slot[...], fm[...]))
    for step in range(2):
        both = found[step * 64 : step * 64 + 32] + found[step * 64 + 32 : step * 64 + 64]
        for o in range(N_SOLID):
            fsend[step, o * 16 : (o + 1) * 16] = both[
                (o & 1) * 16 : (o & 1) * 16 + 16, (o >> 1) * 128 : (o >> 1) * 128 + 128
            ]
    flux_copies = []
    for d in range(1, N_SOLID):
        to = (so + d) & (N_SOLID - 1)
        flux_copies.append(
            pltpu.make_async_remote_copy(
                src_ref=fsend.at[:, pl.ds(pl.multiple_of(to * 16, 16), 16)],
                dst_ref=frecv.at[:, pl.ds(pl.multiple_of(so * 16, 16), 16)],
                send_sem=f_send_sem.at[d - 1],
                recv_sem=f_recv_sem.at[d - 1],
                device_id={"solid": to},
                device_id_type=MESH,
            )
        )
    for copy in flux_copies:
        copy.start()
    own = pl.multiple_of(so * 16, 16)
    for step in range(2):
        frecv[step, pl.ds(own, 16)] = fsend[step, pl.ds(own, 16)]

    merged_1 = receive_halos(1, halos_1, q1)

    def second(x, _):
        rows = pl.ds(pl.multiple_of(x * CY, CY), CY)
        centre, fresh = advanced(q1, merged_1, x)
        u, v, w, temp = centre
        total = transfer_of(u, v, w) * (count[rows, :] * temp - later[rows, :])
        fresh[3] = fresh[3] - WALL_WEIGHT * total
        for c in range(NV):
            out_state[c, x] = fresh[c]
        return 0

    lax.fori_loop(0, XL, second, 0, unroll=16)
    flux_arrivals()
    out_flux[...] = frecv[...]
    for copy in wall_copies + precursor_copies + halos_0 + halos_1 + flux_copies:
        copy.wait_send()


def finish(fluid, fv, wall, out_state, out_wall, wv, out_sem):
    outs = [pltpu.make_async_copy(fluid.at[c], out_state.at[c], out_sem.at[c]) for c in range(NV)]
    for copy in outs:
        copy.start()
    layer = iota((LAYERS, 128), 0)

    def conduct(temps, flux_row):
        conductivity = jnp.exp(CONDUCT_SLOPE * temps)
        above = pltpu.roll(temps, LAYERS - 1, 0)
        c_above = pltpu.roll(conductivity, LAYERS - 1, 0)
        flow = jnp.where(
            layer == LAYERS - 1,
            conductivity * (0.0 - temps),
            0.5 * (conductivity + c_above) * (above - temps),
        )
        from_below = jnp.where(layer == 0, flux_row, -pltpu.roll(flow, 1, 0))
        return temps + SOLID_STEP * (flow + from_below)

    for part in range(4):
        cols = [slice((part * 16 + i) * 128, (part * 16 + i + 1) * 128) for i in range(16)]
        temps = [wall[:, col] for col in cols]
        for step in range(2):
            rows = [fv[step, part * 16 + i : part * 16 + i + 1, :] for i in range(16)]
            temps = [conduct(temp, flux_row) for temp, flux_row in zip(temps, rows)]
        for col, temp in zip(cols, temps):
            wv[:, col] = temp
        span = slice(part * 2048, (part + 1) * 2048)
        outs.append(pltpu.make_async_copy(wv.at[:, span], out_wall.at[:, span], out_sem.at[NV + part]))
        outs[-1].start()
    for copy in outs:
        copy.wait()


def local(state, precursor, inlet_map, face_cell, face_owner, wall_temp):
    any_space = pl.BlockSpec(memory_space=pl.ANY)
    vmem = pltpu.VMEM
    dma = pltpu.SemaphoreType.DMA
    fluid, flux = pl.pallas_call(
        kernel,
        out_shape=(vmem((NV, XL, CY, CZ), F32), vmem((2, 64, 128), F32)),
        in_specs=[any_space] * 6,
        out_specs=(pl.BlockSpec(memory_space=vmem),) * 2,
        scratch_shapes=[
            vmem((NV, XL + 2, PITCH, CZ), F32),
            vmem((NV, XL + 2, PITCH, CZ), F32),
            vmem((LAYERS, COLUMNS), F32),
            vmem((2, NV, CAP), BF16),
            vmem((CY, CZ), I32),
            vmem((ROWS, 128), I32),
            vmem((ROWS, 128), I32),
            vmem((2, 64, 128), F32),
            vmem((2, N_INFLOW, 64, 128), BF16),
            vmem((128, 128), F32),
            vmem((128, 128), F32),
            vmem((2, 2, 128, 128), F32),
            vmem((2, 2, 128, 128), F32),
            vmem((2, 2, CY, 128), F32),
            vmem((2, 2, 2, CY, 128), F32),
            vmem((2, 64, 128), F32),
            vmem((2, 64, 128), F32),
            vmem((512, FACES), BF16),
            vmem((256, FACES), BF16),
            vmem((256, CY * CZ), BF16),
            vmem((32, FACES), BF16),
            vmem((640, FACES), BF16),
            vmem((128, FACES), BF16),
            vmem((4, 512, 128), BF16),
            vmem((4, 512, 128), BF16),
            vmem((128, 256), BF16),
            vmem((ROWS, 128), F32),
            vmem((ROWS, 128), F32),
            vmem((ROWS, 128), F32),
            vmem((ROWS, 128), F32),
            vmem((ROWS, 128), F32),
            vmem((ROWS, 128), F32),
            vmem((CY, 128), F32),
            vmem((CY, 128), F32),
            vmem((CY, 128), I32),
            vmem((ROWS, 128), I32),
            vmem((ROWS, 128), I32),
            vmem((512, 128), F32),
            vmem((512, 128), F32),
            vmem((512, 128), F32),
            vmem((512, 128), F32),
            vmem((ROWS, 128), F32),
            vmem((ROWS, 128), F32),
            vmem((ROWS, 128), F32),
            vmem((ROWS, 128), F32),
            vmem((ROWS, 128), F32),
            vmem((256, CHUNK), F32),
            vmem((256, CHUNK), F32),
            dma((6,)),
            dma((N_INFLOW - 1,)),
            dma((N_INFLOW - 1,)),
            dma((N_SOLID - 1,)),
            dma((N_SOLID - 1,)),
            dma((2, 2, 2)),
            dma((2, 2, 2)),
            dma((N_SOLID - 1,)),
            dma((N_SOLID - 1,)),
        ],
        compiler_params=pltpu.CompilerParams(
            collective_id=0, has_side_effects=True, vmem_limit_bytes=60 * 1024 * 1024
        ),
        name="manifold_step",
    )(
        state[0],
        precursor[0],
        inlet_map[0],
        face_cell.reshape(ROWS, 128),
        face_owner.reshape(ROWS, 128),
        wall_temp[0, 0, 0],
    )
    new_state, new_wall = pl.pallas_call(
        finish,
        out_shape=(
            jax.ShapeDtypeStruct((NV, XL, CY, CZ), F32),
            jax.ShapeDtypeStruct((LAYERS, COLUMNS), F32),
        ),
        in_specs=[any_space] + [pl.BlockSpec(memory_space=vmem)] * 2,
        out_specs=(any_space, any_space),
        scratch_shapes=[
            vmem((LAYERS, COLUMNS), F32),
            dma((2 * NV,)),
        ],
        compiler_params=pltpu.CompilerParams(vmem_limit_bytes=8 * 1024 * 1024),
        name="finish",
    )(fluid, flux, wall_temp[0, 0, 0])
    return new_state[None], new_wall[None, None, None]


def solution(mesh):
    return jax.shard_map(
        local,
        mesh=mesh,
        in_specs=(
            P("solid", None, None, "fluid", "inflow"),
            P("solid", None, None, ("fluid", "inflow")),
            P("solid", "fluid", "inflow"),
            P("solid", "fluid", "inflow", None),
            P("solid", "fluid", "inflow", None, None),
            P("solid", "fluid", "inflow", None, None),
        ),
        out_specs=(
            P("solid", None, None, "fluid", "inflow"),
            P("solid", "fluid", "inflow", None, None),
        ),
        check_vma=False,
    )
```

```python
import functools

import jax
import jax.numpy as jnp
from jax import lax
from jax.experimental import pallas as pl
from jax.experimental.pallas import tpu as pltpu
from jax.sharding import PartitionSpec as P

F32, BF16, I32 = jnp.float32, jnp.bfloat16, jnp.int32
MESH = pl.DeviceIdType.MESH

XL, CY, CZ, NV = 32, 16, 128, 4
CAP, LAYERS, FACES = 2048, 8, 4096
N_FLUID, N_INFLOW, N_SOLID = 8, 8, 4
COLUMNS = N_SOLID * CAP
ROWS = FACES // 128
TOP, PITCH = 8, 32
CHUNK = 512
CHUNKS = FACES // CHUNK
PLANES = XL // CHUNKS

TIME_STEP = 0.1
VISCOSITY = 0.5
HEAT_TRANSFER = 0.8
CONDUCT_SLOPE = 0.2
SOLID_STEP = 0.15
WALL_WEIGHT = 0.5


def split(x):
    high = x.astype(BF16)
    return high, (x - high.astype(F32)).astype(BF16)


def transfer_of(u, v, w):
    return HEAT_TRANSFER * (1.0 + 0.5 * (u * u + v * v + w * w))


def iota(shape, dim):
    return lax.broadcasted_iota(I32, shape, dim)


def bits(mask):
    return jnp.where(mask, 1.0, 0.0).astype(BF16)


def dot(a, b):
    return lax.dot_general(a, b, (((1,), (0,)), ((), ())), preferred_element_type=F32)


def dot_t(a, b):
    return lax.dot_general(a, b, (((1,), (1,)), ((), ())), preferred_element_type=F32)


def kernel(
    state,
    prec,
    imap,
    fcell,
    fown,
    wall,
    out_state,
    out_flux,
    q0,
    q1,
    wv,
    pv,
    imv,
    fcv,
    fov,
    psend,
    win,
    wsend,
    wrecv,
    hy_send,
    hy_recv,
    hz_send,
    hz_recv,
    fsend,
    frecv,
    oh_cell,
    oh_slot,
    oh_in,
    oh_srow,
    vm,
    fm,
    lhs_0,
    lhs_1,
    wl,
    zf,
    qf,
    rf,
    lf,
    hf,
    sf,
    zi,
    hi_in,
    ri,
    rcell,
    rslot,
    count,
    s_sum,
    f_sum,
    later,
    a_face,
    b_face,
    t_face,
    i_face,
    f_face,
    found_0,
    found_1,
    load_sem,
    p_send_sem,
    p_recv_sem,
    w_send_sem,
    w_recv_sem,
    h_send_sem,
    h_recv_sem,
    f_send_sem,
    f_recv_sem,
):
    fl, inf, so = lax.axis_index("fluid"), lax.axis_index("inflow"), lax.axis_index("solid")

    loads = [
        pltpu.make_async_copy(prec, pv, load_sem.at[0]),
        pltpu.make_async_copy(wall, wv, load_sem.at[1]),
        pltpu.make_async_copy(fown, fov, load_sem.at[3]),
        pltpu.make_async_copy(fcell, fcv, load_sem.at[4]),
        pltpu.make_async_copy(imap, imv, load_sem.at[5]),
        pltpu.make_async_copy(state, q0.at[:, pl.ds(1, XL), pl.ds(TOP, CY)], load_sem.at[2]),
    ]

    barrier = pltpu.get_barrier_semaphore()

    def greet(ids):
        pl.semaphore_signal(barrier, inc=1, device_id=ids, device_id_type=MESH)

    for d in range(1, N_INFLOW):
        greet({"inflow": (inf + d) & (N_INFLOW - 1)})
    for d in (1, N_FLUID - 1):
        greet({"fluid": (fl + d) & (N_FLUID - 1)})
    for d in range(1, N_SOLID):
        greet({"solid": (so + d) & (N_SOLID - 1)})

    for load in loads:
        load.start()

    lane = iota((CY, CZ), 1)

    loads[0].wait()
    for s in range(2):
        for k in range(16):
            psend[s, pl.ds(k, 4, stride=16), :] = pv[s, :, k * 128 : (k + 1) * 128].astype(F32)
    for s in range(2):
        win[s, inf] = psend[s].astype(BF16)
    loads[1].wait()
    for t in range(64):
        wsend[pl.ds(t // 16 * 32 + t % 16, 2, stride=16), :] = wv[0:2, t * 128 : (t + 1) * 128]

    wall_copies = []
    for d in range(1, N_SOLID):
        to = (so + d) & (N_SOLID - 1)
        wall_copies.append(
            pltpu.make_async_remote_copy(
                src_ref=wsend.at[pl.ds(pl.multiple_of(to * 32, 32), 32)],
                dst_ref=wrecv.at[pl.ds(pl.multiple_of(so * 32, 32), 32)],
                send_sem=w_send_sem.at[d - 1],
                recv_sem=w_recv_sem.at[d - 1],
                device_id={"solid": to},
                device_id_type=MESH,
            )
        )

    def halo_copies(step):
        copies = []
        for side in range(2):
            far = N_FLUID - 1 if side == 0 else 1
            copies.append(
                pltpu.make_async_remote_copy(
                    src_ref=hy_send.at[step, side],
                    dst_ref=hy_recv.at[step, 1 - side],
                    send_sem=h_send_sem.at[step, 0, side],
                    recv_sem=h_recv_sem.at[step, 0, side],
                    device_id={"fluid": (fl + far) & (N_FLUID - 1)},
                    device_id_type=MESH,
                )
            )
        for side in range(2):
            far = N_INFLOW - 1 if side == 0 else 1
            copies.append(
                pltpu.make_async_remote_copy(
                    src_ref=hz_send.at[step],
                    dst_ref=hz_recv.at[step, 1 - side],
                    send_sem=h_send_sem.at[step, 1, side],
                    recv_sem=h_recv_sem.at[step, 1, side],
                    device_id={"inflow": (inf + far) & (N_INFLOW - 1)},
                    device_id_type=MESH,
                )
            )
        return copies

    precursor_copies = [
        pltpu.make_async_remote_copy(
            src_ref=win.at[:, inf],
            dst_ref=win.at[:, inf],
            send_sem=p_send_sem.at[d - 1],
            recv_sem=p_recv_sem.at[d - 1],
            device_id={"inflow": (inf + d) & (N_INFLOW - 1)},
            device_id_type=MESH,
        )
        for d in range(1, N_INFLOW)
    ]

    def precursor_arrivals():
        for d in range(1, N_INFLOW):
            came = (inf + N_INFLOW - d) & (N_INFLOW - 1)
            pltpu.make_async_remote_copy(
                src_ref=win.at[:, came],
                dst_ref=win.at[:, came],
                send_sem=p_send_sem.at[d - 1],
                recv_sem=p_recv_sem.at[d - 1],
                device_id={"inflow": came},
                device_id_type=MESH,
            ).wait_recv()

    def wall_arrivals():
        for d in range(1, N_SOLID):
            came = (so + N_SOLID - d) & (N_SOLID - 1)
            pltpu.make_async_remote_copy(
                src_ref=wsend.at[pl.ds(pl.multiple_of(came * 32, 32), 32)],
                dst_ref=wrecv.at[pl.ds(pl.multiple_of(came * 32, 32), 32)],
                send_sem=w_send_sem.at[d - 1],
                recv_sem=w_recv_sem.at[d - 1],
                device_id={"solid": came},
                device_id_type=MESH,
            ).wait_recv()

    def flux_arrivals():
        for d in range(1, N_SOLID):
            came = (so + N_SOLID - d) & (N_SOLID - 1)
            pltpu.make_async_remote_copy(
                src_ref=fsend.at[:, pl.ds(pl.multiple_of(came * 16, 16), 16)],
                dst_ref=frecv.at[:, pl.ds(pl.multiple_of(came * 16, 16), 16)],
                send_sem=f_send_sem.at[d - 1],
                recv_sem=f_recv_sem.at[d - 1],
                device_id={"solid": came},
                device_id_type=MESH,
            ).wait_recv()

    for load in loads[2:5]:
        load.wait()
    cell = fcv[...]
    qf[...] = lax.shift_right_logical(cell, 14).astype(F32)
    zf[...] = (cell & 127).astype(F32)
    r = lax.shift_right_logical(cell, 7) & 127
    rcell[...] = r
    rf[...] = r.astype(F32)
    owner = fov[...]
    marks = jnp.concatenate([jnp.where(owner == o, 1.0, 0.0) for o in range(N_SOLID)], axis=0)
    upper = jnp.where(iota((128, 128), 0) < iota((128, 128), 1), 1.0, 0.0)
    earlier = dot(
        marks.astype(BF16), jnp.concatenate([upper, jnp.ones((128, 128), F32)], axis=1).astype(BF16)
    )
    r_out, r_in = iota((128, 128), 0), iota((128, 128), 1)
    same = lax.shift_right_logical(r_out, 5) == lax.shift_right_logical(r_in, 5)
    below = bits(jnp.logical_and(same, r_in < r_out))
    ranks = (earlier[:, :128] + dot(below, earlier[:, 128:].astype(BF16))) * marks
    rank = ranks[0:32] + ranks[32:64] + ranks[64:96] + ranks[96:128]
    slot = owner * CAP + rank.astype(I32)
    hi = lax.shift_right_logical(slot, 7)
    hf[...] = lax.shift_right_logical(hi, 5).astype(F32)
    lf[...] = (slot & 127).astype(F32)
    rslot[...] = hi & 31
    sf[...] = (hi & 31).astype(F32)
    relative = imv[...] - fl * (N_INFLOW * CAP)
    hi = lax.shift_right_logical(relative, 7)
    zi[...] = (relative & 127).astype(F32)
    hi_in[...] = lax.shift_right_logical(hi, 6).astype(F32)
    ri[...] = hi & 63

    steps_128 = iota((128, 128), 0).astype(F32).astype(BF16)
    one, zero = jnp.ones((), BF16), jnp.zeros((), BF16)

    def wide(row_values, blocks):
        tile = jnp.broadcast_to(row_values, (16, 128)).astype(BF16)
        return jnp.concatenate([tile] * blocks, axis=0) if blocks > 1 else tile

    def hot(row_values, blocks):
        return jnp.where(steps_128[: blocks * 16] == wide(row_values, blocks), one, zero)

    def marked(row_values, value, blocks):
        return wide(jnp.where(row_values == value, 1.0, 0.0), blocks)

    def lanes_of(j):
        return pl.ds(pl.multiple_of(j * 128, 128), 128)

    def one_hots_of_faces(j):
        at, cols = pl.ds(j, 1), lanes_of(j)
        base, quarter = hot(zf[at, :], 8), qf[at, :]
        for part in range(4):
            oh_cell[part * 128 : (part + 1) * 128, cols] = base * marked(quarter, float(part), 8)
        vm[0:128, cols] = hot(rf[at, :], 8)
        base, half = hot(lf[at, :], 8), hf[at, :]
        for part in range(2):
            oh_slot[part * 128 : (part + 1) * 128, cols] = base * marked(half, float(part), 8)
        oh_srow[:, cols] = hot(sf[at, :], 2)

    def one_hots_of_inlet(j):
        at, cols = slice(j, j + 1), slice(j * 128, (j + 1) * 128)
        base, half = hot(zi[at, :], 8), hi_in[at, :]
        for part in range(2):
            oh_in[part * 128 : (part + 1) * 128, cols] = base * marked(half, float(part), 8)

    for j in range(CY):
        one_hots_of_inlet(j)

    pl.semaphore_wait(barrier, (N_INFLOW - 1) + 2 + (N_SOLID - 1))
    for copy in wall_copies + precursor_copies:
        copy.start()

    def pair_of(c, x):
        return (c % 2) * XL + x

    def keep_edges(step, x, values, packed):
        packed = list(packed)
        for c in range(NV):
            k = c * XL + x
            hy_send[step, 0, pl.ds(k, 1), :] = values[c][0:1]
            hy_send[step, 1, pl.ds(k, 1), :] = values[c][CY - 1 : CY]
            j = pair_of(c, x)
            moved = pltpu.roll(values[c], 2 * j + 1, 1)
            packed[c // 2] = jnp.where(lax.shift_right_logical(lane, 1) == j, moved, packed[c // 2])
        return tuple(packed)

    zero_plane = jnp.zeros((CY, CZ), F32)
    lhs = (lhs_0, lhs_1)

    def keep_sample_plane(step, x, u, v, w, temp):
        (a_high, a_low), (b_high, b_low) = split(transfer_of(u, v, w)), split(temp)
        parts = (a_high, b_high, a_low, b_low)
        quarter = lax.shift_right_logical(x, 3)
        at = pl.multiple_of((x & 7) * CY, CY)
        for i, part in enumerate(parts):
            lhs[step][quarter, pl.ds(i * 128 + at, CY), :] = part

    loads[5].wait()

    def prepare(n, packed):
        for i in range(4):
            x = n * 4 + i
            values = [q0[c, x + 1, TOP : TOP + CY, :] for c in range(NV)]
            keep_sample_plane(0, x, *values)
            packed = keep_edges(0, x, values, packed)
            one_hots_of_faces(n * 4 + i)
        return packed

    packed = lax.fori_loop(0, XL // 4, prepare, (zero_plane, zero_plane), unroll=4)
    hz_send[0, 0] = packed[0]
    hz_send[0, 1] = packed[1]
    halos_0 = halo_copies(0)
    for copy in halos_0:
        copy.start()
    for c in range(NV):
        q0[c, XL + 1, TOP : TOP + CY, :] = q0[c, XL, TOP : TOP + CY, :]

    def sample_product(step, n, found):
        cols = oh_cell[:, pl.ds(pl.multiple_of(n * CHUNK, CHUNK), CHUNK)]
        fields = jnp.concatenate([lhs[step][i] for i in range(4)], axis=1)
        both = dot(fields, cols)
        found[...] = both[0:256] + both[256:512]

    def sample_pick(n, found):
        for j in range(CHUNK // 128):
            at = n * (CHUNK // 128) + j
            cols = slice(j * 128, (j + 1) * 128)
            mask = iota((128, 128), 0) == rcell[pl.ds(at, 1), :]
            for ref, base in ((a_face, 0), (b_face, 128)):
                both = found[base : base + 128, cols]
                ref[pl.ds(at, 1), :] = jnp.sum(jnp.where(mask, both, 0.0), axis=0, keepdims=True)

    def sample_faces(step, beside, carry):
        sample_product(step, 0, found_0)

        def two(m, carry):
            sample_product(step, 2 * m + 1, found_1)
            carry = beside(2 * m, carry)
            sample_pick(2 * m, found_0)
            sample_product(step, (2 * m + 2) & (CHUNKS - 1), found_0)
            carry = beside(2 * m + 1, carry)
            sample_pick(2 * m + 1, found_1)
            return carry

        return lax.fori_loop(0, CHUNKS // 2, two, carry, unroll=CHUNKS // 2 if step == 0 else 2)

    own = pl.multiple_of(so * 32, 32)
    wrecv[pl.ds(own, 32)] = wsend[pl.ds(own, 32)]
    wall_arrivals()
    for o in range(N_SOLID):
        for layer in range(2):
            for i, part in enumerate(split(wrecv[o * 32 + layer * 16 : o * 32 + layer * 16 + 16, :])):
                at = (layer * 2 + i) * 32 + (o & 1) * 16
                wl[at : at + 16, (o >> 1) * 128 : (o >> 1) * 128 + 128] = part

    for n in range(FACES // 512):
        found = dot(wl[...], oh_slot[:, n * 512 : (n + 1) * 512])
        for j in range(4):
            at = n * 4 + j
            mask = iota((32, 128), 0) == rslot[at : at + 1, :]
            part = found[:, j * 128 : (j + 1) * 128]
            for ref, base in ((t_face, 0), (i_face, 64)):
                both = part[base : base + 32] + part[base + 32 : base + 64]
                ref[at : at + 1, :] = jnp.sum(jnp.where(mask, both, 0.0), axis=0, keepdims=True)
    t0 = t_face[...]
    t1 = i_face[...]
    between = 0.5 * (jnp.exp(CONDUCT_SLOPE * t0) + jnp.exp(CONDUCT_SLOPE * t1)) * (t1 - t0)
    i_face[...] = between

    def halves(x):
        high, low = split(x)
        return high.astype(F32), low.astype(F32)

    fields = halves(t0) + halves(between)
    for j in range(ROWS):
        cols = slice(j * 128, (j + 1) * 128)
        marks = vm[0:128, cols]
        for i, field in enumerate(fields):
            vm[(i + 1) * 128 : (i + 2) * 128, cols] = marks * wide(field[j : j + 1, :], 8)
    sums = dot_t(vm[...], oh_cell[...])
    for part in range(4):
        cols, rows = slice(part * 128, (part + 1) * 128), slice(part * 128, (part + 1) * 128)
        count[rows, :] = sums[0:128, cols]
        s_sum[rows, :] = sums[128:256, cols] + sums[256:384, cols]
        f_sum[rows, :] = sums[384:512, cols] + sums[512:640, cols]

    precursor_arrivals()
    window = jnp.concatenate(
        [
            jnp.concatenate(
                [win[step, 0:4].reshape(256, 128), win[step, 4:8].reshape(256, 128)], axis=1
            )
            for step in range(2)
        ],
        axis=0,
    )
    for g in range(CY // 4):
        found = dot(window, oh_in[:, g * 512 : (g + 1) * 512])
        for j in range(4):
            y = g * 4 + j
            mask = iota((64, 128), 0) == ri[y : y + 1, :]
            for step, dst in ((0, q0), (1, q1)):
                part = found[step * 256 : (step + 1) * 256, j * 128 : (j + 1) * 128]
                for c in range(NV):
                    total = None
                    for src in range(4):
                        term = jnp.where(
                            mask[src * 16 : src * 16 + 16],
                            part[src * 64 + c * 16 : src * 64 + c * 16 + 16],
                            0.0,
                        )
                        total = term if total is None else total + term
                    dst[c, 0, TOP + y : TOP + y + 1, :] = jnp.sum(total, axis=0, keepdims=True)

    def receive_halos(step, copies, dst):
        for copy in copies:
            copy.wait_recv()

        def rows_of(x, _):
            for c in range(NV):
                k = c * XL + x
                dst[c, x + 1, TOP - 1 : TOP, :] = jnp.where(
                    fl > 0, hy_recv[step, 0, pl.ds(k, 1), :], 0.0
                )
                dst[c, x + 1, TOP + CY : TOP + CY + 1, :] = jnp.where(
                    fl < N_FLUID - 1, hy_recv[step, 1, pl.ds(k, 1), :], 0.0
                )
            return 0

        lax.fori_loop(0, XL, rows_of, 0, unroll=32)
        merged = []
        for part in range(2):
            low = jnp.where(inf > 0, pltpu.roll(hz_recv[step, 0, part], 1, 1), 0.0)
            high = jnp.where(inf < N_INFLOW - 1, pltpu.roll(hz_recv[step, 1, part], 127, 1), 0.0)
            merged.append(jnp.where((lane & 1) == 1, low, high))
        return merged

    first_lane, last_lane = lane == 0, lane == CZ - 1

    def advanced(src, merged, x):
        centre = [src[c, x + 1, TOP : TOP + CY, :] for c in range(NV)]
        half = 0.5 * TIME_STEP
        slopes = [half * speed for speed in centre[:3]]
        ahead = [VISCOSITY * TIME_STEP - slope for slope in slopes]
        behind = [VISCOSITY * TIME_STEP + slope for slope in slopes]
        fresh = []
        for c in range(NV):
            q = centre[c]
            j = pair_of(c, x)
            edge = pltpu.roll(merged[c // 2], 127 - 2 * j, 1)
            zm = jnp.where(first_lane, edge, pltpu.roll(q, 1, 1))
            zp = jnp.where(last_lane, edge, pltpu.roll(q, CZ - 1, 1))
            xm = src[c, x, TOP : TOP + CY, :]
            xp = src[c, x + 2, TOP : TOP + CY, :]
            ym = src[c, x + 1, TOP - 1 : TOP + CY - 1, :]
            yp = src[c, x + 1, TOP + 1 : TOP + CY + 1, :]
            along_x = ahead[0] * xp + behind[0] * xm
            along_y = ahead[1] * yp + behind[1] * ym
            along_z = ahead[2] * zp + behind[2] * zm
            fresh.append(
                (1.0 - 6.0 * VISCOSITY * TIME_STEP) * q + ((along_x + along_y) + along_z)
            )
        return centre, fresh

    merged_0 = receive_halos(0, halos_0, q0)

    def first(n, packed):
        for i in range(PLANES):
            x = n * PLANES + i
            rows = pl.ds(pl.multiple_of(x * CY, CY), CY)
            centre, fresh = advanced(q0, merged_0, x)
            u, v, w, temp = centre
            colder = s_sum[rows, :]
            total = transfer_of(u, v, w) * (count[rows, :] * temp - colder)
            later[rows, :] = colder + SOLID_STEP * (f_sum[rows, :] + total)
            fresh[3] = fresh[3] - WALL_WEIGHT * total
            for c in range(NV):
                q1[c, x + 1, TOP : TOP + CY, :] = fresh[c]
            keep_sample_plane(1, x, *fresh)
            packed = keep_edges(1, x, fresh, packed)
        return packed

    packed = sample_faces(0, first, (zero_plane, zero_plane))
    hz_send[1, 0] = packed[0]
    hz_send[1, 1] = packed[1]
    halos_1 = halo_copies(1)
    for copy in halos_1:
        copy.start()
    for c in range(NV):
        q1[c, XL + 1, TOP : TOP + CY, :] = q1[c, XL, TOP : TOP + CY, :]

    flux_0 = a_face[...] * (b_face[...] - t_face[...])
    t_face[...] = t_face[...] + SOLID_STEP * (i_face[...] + flux_0)
    f_face[...] = flux_0
    sample_faces(1, lambda n, carry: carry, 0)
    parts = halves(f_face[...]) + halves(a_face[...] * (b_face[...] - t_face[...]))
    for j in range(ROWS):
        cols = slice(j * 128, (j + 1) * 128)
        marks = oh_srow[:, cols]
        for i, part in enumerate(parts):
            fm[i * 32 : (i + 1) * 32, cols] = marks * wide(part[j : j + 1, :], 2)
    found = jnp.transpose(dot_t(oh_slot[...], fm[...]))
    for step in range(2):
        both = found[step * 64 : step * 64 + 32] + found[step * 64 + 32 : step * 64 + 64]
        for o in range(N_SOLID):
            fsend[step, o * 16 : (o + 1) * 16] = both[
                (o & 1) * 16 : (o & 1) * 16 + 16, (o >> 1) * 128 : (o >> 1) * 128 + 128
            ]
    flux_copies = []
    for d in range(1, N_SOLID):
        to = (so + d) & (N_SOLID - 1)
        flux_copies.append(
            pltpu.make_async_remote_copy(
                src_ref=fsend.at[:, pl.ds(pl.multiple_of(to * 16, 16), 16)],
                dst_ref=frecv.at[:, pl.ds(pl.multiple_of(so * 16, 16), 16)],
                send_sem=f_send_sem.at[d - 1],
                recv_sem=f_recv_sem.at[d - 1],
                device_id={"solid": to},
                device_id_type=MESH,
            )
        )
    for copy in flux_copies:
        copy.start()
    own = pl.multiple_of(so * 16, 16)
    for step in range(2):
        frecv[step, pl.ds(own, 16)] = fsend[step, pl.ds(own, 16)]

    merged_1 = receive_halos(1, halos_1, q1)

    def second(x, _):
        rows = pl.ds(pl.multiple_of(x * CY, CY), CY)
        centre, fresh = advanced(q1, merged_1, x)
        u, v, w, temp = centre
        total = transfer_of(u, v, w) * (count[rows, :] * temp - later[rows, :])
        fresh[3] = fresh[3] - WALL_WEIGHT * total
        for c in range(NV):
            out_state[c, x] = fresh[c]
        return 0

    lax.fori_loop(0, XL, second, 0, unroll=16)
    flux_arrivals()
    out_flux[...] = frecv[...]
    for copy in wall_copies + precursor_copies + halos_0 + halos_1 + flux_copies:
        copy.wait_send()


def finish(fluid, fv, wall, out_state, out_wall, wv, out_sem):
    outs = [pltpu.make_async_copy(fluid.at[c], out_state.at[c], out_sem.at[c]) for c in range(NV)]
    for copy in outs:
        copy.start()
    layer = iota((LAYERS, 128), 0)

    def conduct(temps, flux_row):
        conductivity = jnp.exp(CONDUCT_SLOPE * temps)
        above = pltpu.roll(temps, LAYERS - 1, 0)
        c_above = pltpu.roll(conductivity, LAYERS - 1, 0)
        flow = jnp.where(
            layer == LAYERS - 1,
            conductivity * (0.0 - temps),
            0.5 * (conductivity + c_above) * (above - temps),
        )
        from_below = jnp.where(layer == 0, flux_row, -pltpu.roll(flow, 1, 0))
        return temps + SOLID_STEP * (flow + from_below)

    for part in range(4):
        cols = [slice((part * 16 + i) * 128, (part * 16 + i + 1) * 128) for i in range(16)]
        temps = [wall[:, col] for col in cols]
        for step in range(2):
            rows = [fv[step, part * 16 + i : part * 16 + i + 1, :] for i in range(16)]
            temps = [conduct(temp, flux_row) for temp, flux_row in zip(temps, rows)]
        for col, temp in zip(cols, temps):
            wv[:, col] = temp
        span = slice(part * 2048, (part + 1) * 2048)
        outs.append(pltpu.make_async_copy(wv.at[:, span], out_wall.at[:, span], out_sem.at[NV + part]))
        outs[-1].start()
    for copy in outs:
        copy.wait()


def local(state, precursor, inlet_map, face_cell, face_owner, wall_temp):
    any_space = pl.BlockSpec(memory_space=pl.ANY)
    vmem = pltpu.VMEM
    dma = pltpu.SemaphoreType.DMA
    fluid, flux = pl.pallas_call(
        kernel,
        out_shape=(vmem((NV, XL, CY, CZ), F32), vmem((2, 64, 128), F32)),
        in_specs=[any_space] * 6,
        out_specs=(pl.BlockSpec(memory_space=vmem),) * 2,
        scratch_shapes=[
            vmem((NV, XL + 2, PITCH, CZ), F32),
            vmem((NV, XL + 2, PITCH, CZ), F32),
            vmem((LAYERS, COLUMNS), F32),
            vmem((2, NV, CAP), BF16),
            vmem((CY, CZ), I32),
            vmem((ROWS, 128), I32),
            vmem((ROWS, 128), I32),
            vmem((2, 64, 128), F32),
            vmem((2, N_INFLOW, 64, 128), BF16),
            vmem((128, 128), F32),
            vmem((128, 128), F32),
            vmem((2, 2, 128, 128), F32),
            vmem((2, 2, 128, 128), F32),
            vmem((2, 2, CY, 128), F32),
            vmem((2, 2, 2, CY, 128), F32),
            vmem((2, 64, 128), F32),
            vmem((2, 64, 128), F32),
            vmem((512, FACES), BF16),
            vmem((256, FACES), BF16),
            vmem((256, CY * CZ), BF16),
            vmem((32, FACES), BF16),
            vmem((640, FACES), BF16),
            vmem((128, FACES), BF16),
            vmem((4, 512, 128), BF16),
            vmem((4, 512, 128), BF16),
            vmem((128, 256), BF16),
            vmem((ROWS, 128), F32),
            vmem((ROWS, 128), F32),
            vmem((ROWS, 128), F32),
            vmem((ROWS, 128), F32),
            vmem((ROWS, 128), F32),
            vmem((ROWS, 128), F32),
            vmem((CY, 128), F32),
            vmem((CY, 128), F32),
            vmem((CY, 128), I32),
            vmem((ROWS, 128), I32),
            vmem((ROWS, 128), I32),
            vmem((512, 128), F32),
            vmem((512, 128), F32),
            vmem((512, 128), F32),
            vmem((512, 128), F32),
            vmem((ROWS, 128), F32),
            vmem((ROWS, 128), F32),
            vmem((ROWS, 128), F32),
            vmem((ROWS, 128), F32),
            vmem((ROWS, 128), F32),
            vmem((256, CHUNK), F32),
            vmem((256, CHUNK), F32),
            dma((6,)),
            dma((N_INFLOW - 1,)),
            dma((N_INFLOW - 1,)),
            dma((N_SOLID - 1,)),
            dma((N_SOLID - 1,)),
            dma((2, 2, 2)),
            dma((2, 2, 2)),
            dma((N_SOLID - 1,)),
            dma((N_SOLID - 1,)),
        ],
        compiler_params=pltpu.CompilerParams(
            collective_id=0, has_side_effects=True, vmem_limit_bytes=60 * 1024 * 1024
        ),
        name="manifold_step",
    )(
        state[0],
        precursor[0],
        inlet_map[0],
        face_cell.reshape(ROWS, 128),
        face_owner.reshape(ROWS, 128),
        wall_temp[0, 0, 0],
    )
    new_state, new_wall = pl.pallas_call(
        finish,
        out_shape=(
            jax.ShapeDtypeStruct((NV, XL, CY, CZ), F32),
            jax.ShapeDtypeStruct((LAYERS, COLUMNS), F32),
        ),
        in_specs=[any_space] + [pl.BlockSpec(memory_space=vmem)] * 2,
        out_specs=(any_space, any_space),
        scratch_shapes=[
            vmem((LAYERS, COLUMNS), F32),
            dma((2 * NV,)),
        ],
        compiler_params=pltpu.CompilerParams(vmem_limit_bytes=8 * 1024 * 1024),
        name="finish",
    )(fluid, flux, wall_temp[0, 0, 0])
    return new_state[None], new_wall[None, None, None]


def solution(mesh):
    return jax.shard_map(
        local,
        mesh=mesh,
        in_specs=(
            P("solid", None, None, "fluid", "inflow"),
            P("solid", None, None, ("fluid", "inflow")),
            P("solid", "fluid", "inflow"),
            P("solid", "fluid", "inflow", None),
            P("solid", "fluid", "inflow", None, None),
            P("solid", "fluid", "inflow", None, None),
        ),
        out_specs=(
            P("solid", None, None, "fluid", "inflow"),
            P("solid", "fluid", "inflow", None, None),
        ),
        check_vma=False,
    )
```
